128 devices in a mesh: section: 4 (over x_hi, core), vocab: 32 (over y, x_lo, z).
Axes of the slice: x: 4 (x_hi: 2, x_lo: 2; x = x_hi * 2 + x_lo), y: 4, z: 4, core: 2. Of those that a mesh axis runs over, the one named last changes fastest.
Arguments:
- token_grad: bfloat16 [32768, 4608], P('vocab', 'section'), may hold values from -6 to 6
- token_ids: int32 [32768], P('vocab'), may hold values from -1 to 519, as said below
- block_counts: int32 [32, 32], P('vocab'), may hold values from 0 to 1, as said below
- hidden: bfloat16 [2048, 4608], P('section'), may hold values from -6 to 6
- dlogits: bfloat16 [2048, 16640], P('section', 'vocab'), may hold values from -0.125 to 0.125
- master: float32 [16640, 4608], P('vocab', 'section'), may hold values from -0.046875 to 0.046875
- moment1: float32 [16640, 4608], P('vocab', 'section'), may hold values from -4 to 4
- moment2: float32 [16640, 4608], P('vocab', 'section'), may hold values from 0.01 to 1
Outputs:
- new_master: float32 [16640, 4608], P('vocab', 'section')
- new_moment1: float32 [16640, 4608], P('vocab', 'section')
- new_moment2: float32 [16640, 4608], P('vocab', 'section')
- refreshed: bfloat16 [16640, 4608], P('vocab')
The draws below stay inside these ranges and needn't reach their ends.
Inputs may be any that keep to these rules, and one draw needn't show every extreme that they name: `block_counts`: row j gives, for each owner in order, how many of sender j's 8 blocks belong to it; each row sums to 8 and sender j's blocks come in owner order; one owner gets 1 block from every sender. `token_ids`: an id is a row among its block's owner's 520 rows, or -1 for a padding row.
All inputs are finite; a program needn't handle non-finite values.
Results may differ from the reference program's by a relative error of at most 0.005.
Values may be sent and summed in bfloat16 or wider, within the bound.
No kernel may reach another device: no remote copies, remote signals or barrier semaphores. Data moves between devices by JAX's collectives and lax.ppermute only.
A program may use at most 128 MiB of HBM per device.

```python
import math
import jax
import jax.numpy as jnp
from jax import lax

D = 4608
VROWS_DEV = 520
BLOCK = 128
BLK_DEV = 8
OWNERS = 32
CAP = 1
V = 16640
TOKENS = 32768
HTOK = 2048


def draw_block_counts(key, part):
    key = jax.random.fold_in(key, 5)
    heat_key, noise_key, favor_key = jax.random.split(key, 3)
    slot_total = OWNERS * CAP
    slot_owner = jnp.arange(slot_total, dtype=jnp.int32) // CAP
    heat_level = jax.random.randint(heat_key, (OWNERS,), 0, 4, dtype=jnp.int32)
    favored = jax.random.randint(favor_key, (), 0, OWNERS, dtype=jnp.int32)
    noise_score = jax.random.randint(noise_key, (OWNERS, slot_total), 0, 4096, dtype=jnp.int32)
    weight = heat_level[slot_owner] * 1024 + 16384 * (slot_owner == favored).astype(jnp.int32)
    slot_score = (weight[None, :] + noise_score) * slot_total + jnp.arange(slot_total, dtype=jnp.int32)[None, :]
    _, chosen = lax.top_k(slot_score, BLK_DEV)
    chosen_owner = slot_owner[chosen]
    owner_list = jnp.arange(OWNERS, dtype=jnp.int32)
    counts = jnp.sum((chosen_owner[:, :, None] == owner_list[None, None, :]).astype(jnp.int32), axis=1)
    return counts.astype(jnp.int32)


def draw_token_ids(key, part):
    key = jax.random.fold_in(key, 9)
    raw_key, offset_key, padded_key = jax.random.split(key, 3)
    raw_index = jax.random.randint(raw_key, (TOKENS,), 0, VROWS_DEV, dtype=jnp.int32)
    skewed = raw_index * raw_index // VROWS_DEV
    offset = jax.random.randint(offset_key, (TOKENS // BLOCK, 1), 0, VROWS_DEV, dtype=jnp.int32)
    local_id = ((skewed.reshape(-1, BLOCK) + offset) % VROWS_DEV).reshape(-1)
    padded = jax.random.randint(padded_key, (TOKENS,), 0, 4, dtype=jnp.int32) == 0
    return jnp.where(padded, -1, local_id).astype(jnp.int32)


def levels(rng, extent, shards, smallest, high):
    factor_of = 1.0
    for axis_at, shards_of in shards:
        draws = jax.random.uniform(jax.random.fold_in(jax.random.fold_in(rng, 6), axis_at), (shards_of,), jnp.float32, smallest / len(shards), high / len(shards))
        factor_of = factor_of * jnp.repeat(jnp.exp(draws), extent[axis_at] // shards_of).reshape((-1,) + (1,) * (len(extent) - 1 - axis_at))
    return factor_of


def noise(stream_key, shape, scale, limit, shards=(), held_as=jnp.bfloat16):
    values = jax.random.normal(stream_key, shape, jnp.float32) * scale
    if len(shards) > 0:
        values = levels(stream_key, shape, shards, -0.22, 0.18) * values
    return jnp.clip(values, min=-limit, max=limit).astype(held_as)


def setup_inputs(seed: int = 0) -> dict:
    splits = jax.random.split(jax.random.key(seed), 9)
    token_grad = noise(splits[0], (TOKENS, D), 1.0, 6.0, ((0, 32), (1, 4)))
    token_ids = draw_token_ids(jax.random.fold_in(splits[8], 71), 0)
    block_counts = draw_block_counts(jax.random.fold_in(splits[8], 71), 0)
    hidden = noise(splits[3], (HTOK, D), 1.0, 6.0, ((0, 4),))
    dlogits = noise(splits[4], (HTOK, V), HTOK ** -0.5, 0.125, ((0, 4), (1, 32)))
    master = noise(splits[5], (V, D), 0.003, 0.046875, ((0, 32), (1, 4)), jnp.float32)
    moment1 = noise(splits[6], (V, D), 0.3, 4.0, ((0, 32), (1, 4)), jnp.float32)
    moment2 = jnp.clip(jnp.exp(math.log(1.0) - 4.6051702 * jax.random.uniform(splits[7], (V, D), jnp.float32) ** levels(splits[7], (V, D), ((0, 32), (1, 4)), -0.2, 0.2)), 0.01, 1.0)
    return {"token_grad": token_grad, "token_ids": token_ids, "block_counts": block_counts, "hidden": hidden, "dlogits": dlogits, "master": master, "moment1": moment1, "moment2": moment2}


beta_first = 0.9
beta_second = 0.999
learn_rate = 0.01
adam_epsilon = 1e-08
first_fix = 1.0 - 0.9 ** 10
second_fix = 1.0 - 0.999 ** 10

def reference(token_grad, token_ids, block_counts, hidden, dlogits, master, moment1, moment2):
    count_ends = jnp.cumsum(block_counts, axis=1).astype(jnp.int32)
    block_index = jnp.arange(BLK_DEV, dtype=jnp.int32)
    owner_of_block = lax.optimization_barrier(jnp.sum((count_ends[:, None, :] <= block_index[None, :, None]).astype(jnp.int32), axis=2))
    row_owner = jnp.repeat(owner_of_block.reshape(-1), BLOCK).astype(jnp.int32)
    slab_id = jnp.where(token_ids >= 0, row_owner * VROWS_DEV + token_ids, V).astype(jnp.int32)
    token_sum = jax.ops.segment_sum(token_grad.astype(jnp.float32), slab_id, num_segments=V + 1)[:V]
    head_grad = jnp.dot(dlogits.T, hidden, preferred_element_type=jnp.float32)
    gradient = token_sum + head_grad
    new_moment1 = beta_first * moment1 + (1.0 - beta_first) * gradient
    new_moment2 = beta_second * moment2 + (1.0 - beta_second) * gradient * gradient
    new_master = master - learn_rate * (new_moment1 / first_fix) / (jnp.sqrt(new_moment2 / second_fix) + adam_epsilon)
    return (new_master, new_moment1, new_moment2, new_master.astype(jnp.bfloat16))
```

```python
import functools

import jax
import jax.numpy as jnp
from jax import lax
from jax.experimental import pallas as pl
from jax.experimental.pallas import tpu as pltpu
from jax.sharding import PartitionSpec as P

BLOCK = 128


beta_first = 0.9
beta_second = 0.999
learn_rate = 0.01
adam_epsilon = 1e-08
first_fix = 1.0 - 0.9**10
second_fix = 1.0 - 0.999**10

CORE = ((0, 1), (1, 0), (2, 3), (3, 2))
ACROSS = ((0, 2), (2, 0), (1, 3), (3, 1))


def head_kernel(place, dlogits_t, hidden_keep, hidden_send, keep, send):
    left = dlogits_t[...]
    keep[0] = jnp.dot(left, hidden_keep[...], preferred_element_type=jnp.float32).astype(
        jnp.bfloat16
    )
    send[0] = jnp.dot(left, hidden_send[...], preferred_element_type=jnp.float32).astype(
        jnp.bfloat16
    )


def head_parts(hidden, dlogits, section, quarter):
    tokens, rows = dlogits.shape
    shape = jax.ShapeDtypeStruct((2, rows, quarter), jnp.bfloat16)
    return pl.pallas_call(
        head_kernel,
        grid_spec=pltpu.PrefetchScalarGridSpec(
            num_scalar_prefetch=1,
            grid=(2,),
            in_specs=[
                pl.BlockSpec((rows, tokens), lambda h, place: (0, 0)),
                pl.BlockSpec((tokens, quarter), lambda h, place: (0, place[0] ^ (2 * h))),
                pl.BlockSpec((tokens, quarter), lambda h, place: (0, place[0] ^ (2 * h + 1))),
            ],
            out_specs=[
                pl.BlockSpec((1, rows, quarter), lambda h, place: (h, 0, 0)),
                pl.BlockSpec((1, rows, quarter), lambda h, place: (h, 0, 0)),
            ],
        ),
        out_shape=[shape, shape],
        compiler_params=pltpu.CompilerParams(vmem_limit_bytes=40 * 1024 * 1024),
        cost_estimate=pl.CostEstimate(
            flops=2 * tokens * rows * 4 * quarter,
            bytes_accessed=2 * (tokens * 4 * quarter + tokens * rows + 4 * rows * quarter),
            transcendentals=0,
        ),
    )(section.reshape(1), dlogits.T, hidden, hidden)


def sum_kernel(width, senders, blocks, owner, got, out, acc):
    step = pl.program_id(0)
    owners, slab_rows, packed = acc.shape

    @pl.when(step == 0)
    def _():
        acc[...] = jnp.zeros_like(acc)

    row = lax.broadcasted_iota(jnp.int32, (slab_rows, BLOCK), 0).astype(jnp.float32)
    for sender in range(senders):
        for block in range(blocks):
            part = got[sender, :, block * BLOCK : (block + 1) * BLOCK]
            ids = part[width : width + 1].astype(jnp.float32) * 32.0
            ids = ids + part[width + 1 : width + 2].astype(jnp.float32) - 1.0
            one_hot = (row == ids).astype(jnp.bfloat16)
            place = owner[(step * senders + sender) * blocks + block]
            acc[place] += lax.dot_general(
                one_hot, part, (((1,), (1,)), ((), ())), preferred_element_type=jnp.float32
            )

    @pl.when(step == pl.num_programs(0) - 1)
    def _():
        shape = (packed, packed)
        down = lax.broadcasted_iota(jnp.int32, shape, 0)
        across = lax.broadcasted_iota(jnp.int32, shape, 1)
        unit = jnp.logical_and(down == across, down < width).astype(jnp.bfloat16)

        def turn(place, carry):
            out[place] = lax.dot_general(
                unit,
                acc[place].astype(jnp.bfloat16),
                (((1,), (1,)), ((), ())),
                preferred_element_type=jnp.float32,
            ).astype(jnp.bfloat16)
            return carry

        lax.fori_loop(0, owners, turn, 0)


def owner_sums(got, owner, slab_rows, width):
    owners, packed, row_total = got.shape
    senders = 4
    blocks = row_total // BLOCK
    return pl.pallas_call(
        functools.partial(sum_kernel, width, senders, blocks),
        grid_spec=pltpu.PrefetchScalarGridSpec(
            num_scalar_prefetch=1,
            grid=(owners // senders,),
            in_specs=[
                pl.BlockSpec((senders, packed, row_total), lambda i, owner: (i, 0, 0)),
            ],
            out_specs=pl.BlockSpec((owners, packed, slab_rows), lambda i, owner: (0, 0, 0)),
            scratch_shapes=[pltpu.VMEM((owners, slab_rows, packed), jnp.float32)],
        ),
        out_shape=jax.ShapeDtypeStruct((owners, packed, slab_rows), jnp.bfloat16),
        compiler_params=pltpu.CompilerParams(vmem_limit_bytes=40 * 1024 * 1024),
        cost_estimate=pl.CostEstimate(
            flops=2 * owners * row_total * slab_rows * packed,
            bytes_accessed=2 * owners * packed * (row_total + slab_rows),
            transcendentals=0,
        ),
    )(owner, got)


def place_kernel(place, own, core, far, diagonal, out, sems):
    quarter = own.shape[1]
    copies = []
    for k, part in enumerate((own, core, far, diagonal)):
        start = pl.multiple_of((place[0] ^ k) * quarter, 128)
        copies.append(
            pltpu.make_async_copy(part, out.at[:, pl.ds(start, quarter)], sems.at[k])
        )
    for copy in copies:
        copy.start()
    for copy in copies:
        copy.wait()


def assemble(section, own, core, far, diagonal):
    rows, quarter = own.shape
    anywhere = pl.BlockSpec(memory_space=pl.ANY)
    return pl.pallas_call(
        place_kernel,
        in_specs=[pl.BlockSpec(memory_space=pltpu.SMEM)] + [anywhere] * 4,
        out_specs=anywhere,
        scratch_shapes=[pltpu.SemaphoreType.DMA((4,))],
        out_shape=jax.ShapeDtypeStruct((rows, 4 * quarter), jnp.bfloat16),
        cost_estimate=pl.CostEstimate(
            flops=0, bytes_accessed=4 * rows * quarter * 4, transcendentals=0
        ),
    )(section.reshape(1), own, core, far, diagonal)


def shards(token_grad, token_ids, block_counts, hidden, dlogits, master, moment1, moment2):
    owners = lax.axis_size("vocab")
    section = lax.axis_index("section").astype(jnp.int32)
    row_total, quarter = token_grad.shape
    blocks = row_total // BLOCK
    slab_rows = master.shape[0]
    width = quarter // owners
    packed = -(-(width + 3) // 8) * 8

    ends = jnp.cumsum(block_counts[0])
    block_owner = jnp.sum(
        (ends[None, :] <= jnp.arange(blocks, dtype=jnp.int32)[:, None]).astype(jnp.int32), axis=1
    )
    row_owner = jnp.repeat(block_owner, BLOCK)
    shifted = token_ids + 1
    line = jnp.arange(owners * packed, dtype=jnp.int32)
    chunk, within = line // packed, line % packed
    select = jnp.logical_and(
        (chunk * width + within)[:, None] == jnp.arange(quarter, dtype=jnp.int32)[None, :],
        (within < width)[:, None],
    ).astype(jnp.bfloat16)
    turned = lax.dot_general(
        select, token_grad, (((1,), (1,)), ((), ())), preferred_element_type=jnp.float32
    )
    inner = within[:, None]
    turned = jnp.where(
        inner == width,
        (shifted // 32).astype(jnp.float32)[None, :],
        jnp.where(
            inner == width + 1,
            (shifted % 32).astype(jnp.float32)[None, :],
            jnp.where(inner == width + 2, row_owner.astype(jnp.float32)[None, :], turned),
        ),
    ).astype(jnp.bfloat16)
    got = lax.all_to_all(
        turned.reshape(owners, packed, row_total), "vocab", split_axis=0, concat_axis=0, tiled=True
    )

    keep, send = head_parts(hidden, dlogits, section, quarter)
    from_core = lax.ppermute(send, "section", CORE)
    near = keep[0].astype(jnp.float32) + from_core[0].astype(jnp.float32)
    onward = (keep[1].astype(jnp.float32) + from_core[1].astype(jnp.float32)).astype(jnp.bfloat16)
    from_far = lax.ppermute(onward, "section", ACROSS)
    head_grad = near + from_far.astype(jnp.float32)

    got_owner = got[:, width + 2, ::BLOCK].astype(jnp.int32).reshape(-1)
    sums = owner_sums(got, got_owner, slab_rows, width)
    back = lax.all_to_all(sums, "vocab", split_axis=0, concat_axis=0, tiled=True)
    token_sum = lax.dot_general(
        back.reshape(owners * packed, slab_rows),
        select,
        (((0,), (0,)), ((), ())),
        preferred_element_type=jnp.float32,
    )
    gradient = token_sum + head_grad
    new_moment1 = beta_first * moment1 + (1.0 - beta_first) * gradient
    new_moment2 = beta_second * moment2 + (1.0 - beta_second) * gradient * gradient
    new_master = master - learn_rate * (new_moment1 / first_fix) / (
        jnp.sqrt(new_moment2 / second_fix) + adam_epsilon
    )
    own = new_master.astype(jnp.bfloat16)
    far = lax.ppermute(own, "section", ACROSS)
    core = lax.ppermute(own, "section", CORE)
    diagonal = lax.ppermute(far, "section", CORE)
    refreshed = assemble(section, own, core, far, diagonal)
    return (new_master, new_moment1, new_moment2, refreshed)


def solution(mesh):
    placed = (
        P("vocab", "section"),
        P("vocab"),
        P("vocab", None),
        P("section", None),
        P("section", "vocab"),
        P("vocab", "section"),
        P("vocab", "section"),
        P("vocab", "section"),
    )
    return jax.shard_map(
        shards,
        mesh=mesh,
        in_specs=placed,
        out_specs=(
            P("vocab", "section"),
            P("vocab", "section"),
            P("vocab", "section"),
            P("vocab", None),
        ),
        check_vma=False,
    )
```

```python
import functools

import jax
import jax.numpy as jnp
from jax import lax
from jax.experimental import pallas as pl
from jax.experimental.pallas import tpu as pltpu
from jax.sharding import PartitionSpec as P

BLOCK = 128
MIB = 1024 * 1024


beta_first = 0.9
beta_second = 0.999
learn_rate = 0.01
adam_epsilon = 1e-08
first_fix = 1.0 - 0.9**10
second_fix = 1.0 - 0.999**10

CORE = ((0, 1), (1, 0), (2, 3), (3, 2))
ACROSS = ((0, 2), (2, 0), (1, 3), (3, 1))


def head_kernel(place, dlogits_t, hidden_keep, hidden_send, keep, send):
    left = dlogits_t[...]
    keep[0] = jnp.dot(left, hidden_keep[...], preferred_element_type=jnp.float32).astype(
        jnp.bfloat16
    )
    send[0] = jnp.dot(left, hidden_send[...], preferred_element_type=jnp.float32).astype(
        jnp.bfloat16
    )


def head_parts(hidden, dlogits, section, quarter):
    tokens, rows = dlogits.shape
    shape = jax.ShapeDtypeStruct((2, rows, quarter), jnp.bfloat16)
    return pl.pallas_call(
        head_kernel,
        grid_spec=pltpu.PrefetchScalarGridSpec(
            num_scalar_prefetch=1,
            grid=(2,),
            in_specs=[
                pl.BlockSpec((rows, tokens), lambda h, place: (0, 0)),
                pl.BlockSpec((tokens, quarter), lambda h, place: (0, place[0] ^ (2 * h))),
                pl.BlockSpec((tokens, quarter), lambda h, place: (0, place[0] ^ (2 * h + 1))),
            ],
            out_specs=[
                pl.BlockSpec((1, rows, quarter), lambda h, place: (h, 0, 0)),
                pl.BlockSpec((1, rows, quarter), lambda h, place: (h, 0, 0)),
            ],
        ),
        out_shape=[shape, shape],
        compiler_params=pltpu.CompilerParams(vmem_limit_bytes=40 * MIB),
        cost_estimate=pl.CostEstimate(
            flops=2 * tokens * rows * 4 * quarter,
            bytes_accessed=2 * (tokens * 4 * quarter + tokens * rows + 4 * rows * quarter),
            transcendentals=0,
        ),
    )(section.reshape(1), dlogits.T, hidden, hidden)


def sum_kernel(senders, blocks, owner, ids, got, out, acc, parts):
    step = pl.program_id(0)
    owners, _, slab_rows = acc.shape

    @pl.when(step == 0)
    def _():
        acc[...] = jnp.zeros_like(acc)

    lane = lax.broadcasted_iota(jnp.int32, (BLOCK, slab_rows), 1).astype(jnp.float32)
    for sender in range(senders):
        columns = ids[sender].T
        for block in range(blocks):
            part = got[sender, :, block * BLOCK : (block + 1) * BLOCK]
            one_hot = (lane == columns[:, block : block + 1]).astype(jnp.bfloat16)
            parts[sender * blocks + block] = jnp.dot(
                part, one_hot, preferred_element_type=jnp.float32
            )
    for at in range(senders * blocks):
        place = owner[step * senders * blocks + at]
        acc[place] += parts[at]

    @pl.when(step == pl.num_programs(0) - 1)
    def _():
        def narrow(place, carry):
            out[place] = acc[place].astype(jnp.bfloat16)
            return carry

        lax.fori_loop(0, owners, narrow, 0)


def owner_sums(got, owner, ids, slab_rows):
    owners, width, row_total = got.shape
    senders = 4
    blocks = row_total // BLOCK
    return pl.pallas_call(
        functools.partial(sum_kernel, senders, blocks),
        grid_spec=pltpu.PrefetchScalarGridSpec(
            num_scalar_prefetch=1,
            grid=(owners // senders,),
            in_specs=[
                pl.BlockSpec((senders, blocks, BLOCK), lambda i, owner: (i, 0, 0)),
                pl.BlockSpec((senders, width, row_total), lambda i, owner: (i, 0, 0)),
            ],
            out_specs=pl.BlockSpec((owners, width, slab_rows), lambda i, owner: (0, 0, 0)),
            scratch_shapes=[
                pltpu.VMEM((owners, width, slab_rows), jnp.float32),
                pltpu.VMEM((senders * blocks, width, slab_rows), jnp.float32),
            ],
        ),
        out_shape=jax.ShapeDtypeStruct((owners, width, slab_rows), jnp.bfloat16),
        compiler_params=pltpu.CompilerParams(vmem_limit_bytes=40 * MIB),
        cost_estimate=pl.CostEstimate(
            flops=2 * owners * row_total * slab_rows * 256,
            bytes_accessed=2 * owners * width * (row_total + slab_rows),
            transcendentals=0,
        ),
    )(owner, ids, got)


def adam_kernel(
    width, back, keep, core, far, master, moment1, moment2, *rest
):
    out_master, out_moment1, out_moment2, out_own, total = rest[-5:]
    step = pl.program_id(0)
    owners, packed, slab_rows = back.shape
    lanes = out_own.shape[1]

    @pl.when(step == 0)
    def _():
        shape = (owners * packed, owners * width)
        line = lax.broadcasted_iota(jnp.int32, shape, 0)
        feature = lax.broadcasted_iota(jnp.int32, shape, 1)
        within = line % packed
        select = jnp.logical_and(
            (line // packed) * width + within == feature, within < width
        ).astype(jnp.bfloat16)
        summed = lax.dot_general(
            back[...].reshape(owners * packed, slab_rows),
            select,
            (((0,), (0,)), ((), ())),
            preferred_element_type=jnp.float32,
        )
        for at in range(owners * width // lanes):
            total[at] = summed[:, at * lanes : (at + 1) * lanes]

    gradient = (
        total[step]
        + keep[0].astype(jnp.float32)
        + core[0].astype(jnp.float32)
        + far[...].astype(jnp.float32)
    )
    first = beta_first * moment1[...] + (1.0 - beta_first) * gradient
    second = beta_second * moment2[...] + (1.0 - beta_second) * gradient * gradient
    fresh = master[...] - learn_rate * (first / first_fix) / (
        jnp.sqrt(second / second_fix) + adam_epsilon
    )
    out_master[...] = fresh
    out_moment1[...] = first
    out_moment2[...] = second
    out_own[...] = fresh.astype(jnp.bfloat16)


def adam(back, width, start, keep, core, far, master, moment1, moment2, earlier=()):
    owners, packed, slab_rows = back.shape
    span = owners * width
    lanes = 128
    first = start // lanes
    tile = pl.BlockSpec((slab_rows, lanes), lambda i: (0, first + i))
    tile0 = pl.BlockSpec((1, slab_rows, lanes), lambda i: (0, 0, first + i))
    whole = jax.ShapeDtypeStruct(master.shape, jnp.float32)
    return pl.pallas_call(
        functools.partial(adam_kernel, width),
        grid=(span // lanes,),
        in_specs=[
            pl.BlockSpec((owners, packed, slab_rows), lambda i: (0, 0, 0)),
            tile0,
            tile0,
            tile,
            tile,
            tile,
            tile,
        ]
        + [pl.BlockSpec(memory_space=pl.ANY)] * len(earlier),
        out_specs=[tile, tile, tile, pl.BlockSpec((slab_rows, lanes), lambda i: (0, i))],
        out_shape=[whole, whole, whole, jax.ShapeDtypeStruct((slab_rows, span), jnp.bfloat16)],
        scratch_shapes=[pltpu.VMEM((span // lanes, slab_rows, lanes), jnp.float32)],
        input_output_aliases={7 + at: at for at in range(len(earlier))},
        compiler_params=pltpu.CompilerParams(vmem_limit_bytes=40 * MIB),
        cost_estimate=pl.CostEstimate(
            flops=2 * owners * packed * span * slab_rows,
            bytes_accessed=slab_rows * span * 32 + 2 * owners * packed * slab_rows,
            transcendentals=slab_rows * span,
        ),
    )(back, keep, core, far, master, moment1, moment2, *earlier)


def place_kernel(count, place, *refs):
    parts, out = refs[:-1], refs[-1]
    quarter = out.shape[1] // 4
    for k in range(4):
        start = (place[0] ^ k) * quarter
        for at in range(count):
            part = parts[k * count + at]
            size = part.shape[1]
            out[:, pl.ds(pl.multiple_of(start, 128), size)] = part[...]
            start = start + size


def assemble(section, pieces):
    count = len(pieces[0])
    rows = pieces[0][0].shape[0]
    quarter = sum(part.shape[1] for part in pieces[0])
    some = 176
    parts = [part for piece in pieces for part in piece]
    return pl.pallas_call(
        functools.partial(place_kernel, count),
        grid_spec=pltpu.PrefetchScalarGridSpec(
            num_scalar_prefetch=1,
            grid=(-(-rows // some),),
            in_specs=[pl.BlockSpec((some, part.shape[1]), lambda i, place: (i, 0)) for part in parts],
            out_specs=pl.BlockSpec((some, 4 * quarter), lambda i, place: (i, 0)),
        ),
        out_shape=jax.ShapeDtypeStruct((rows, 4 * quarter), jnp.bfloat16),
        compiler_params=pltpu.CompilerParams(vmem_limit_bytes=40 * MIB),
        cost_estimate=pl.CostEstimate(
            flops=0, bytes_accessed=4 * rows * quarter * 4, transcendentals=0
        ),
    )(section.reshape(1), *parts)


def exchange(rows):
    return lax.all_to_all(rows, "vocab", split_axis=0, concat_axis=0, tiled=True)


def shards(token_grad, token_ids, block_counts, hidden, dlogits, master, moment1, moment2):
    owners = lax.axis_size("vocab")
    section = lax.axis_index("section").astype(jnp.int32)
    row_total, quarter = token_grad.shape
    blocks = row_total // BLOCK
    slab_rows = master.shape[0]
    second_width = 16
    first_width = quarter // owners - second_width
    first_span = first_width * owners
    packed = -(-(first_width + 3) // 8) * 8

    ends = jnp.cumsum(block_counts[0])
    block_owner = jnp.sum(
        (ends[None, :] <= jnp.arange(blocks, dtype=jnp.int32)[:, None]).astype(jnp.int32), axis=1
    )
    row_owner = jnp.repeat(block_owner, BLOCK)
    shifted = token_ids + 1
    line = jnp.arange(owners * packed, dtype=jnp.int32)
    chunk, within = line // packed, line % packed
    select = jnp.logical_and(
        (chunk * first_width + within)[:, None]
        == jnp.arange(first_span, dtype=jnp.int32)[None, :],
        (within < first_width)[:, None],
    ).astype(jnp.bfloat16)
    turned = lax.dot_general(
        select,
        token_grad[:, :first_span],
        (((1,), (1,)), ((), ())),
        preferred_element_type=jnp.float32,
    )
    inner = within[:, None]
    turned = jnp.where(
        inner == first_width,
        (shifted // 32).astype(jnp.float32)[None, :],
        jnp.where(
            inner == first_width + 1,
            (shifted % 32).astype(jnp.float32)[None, :],
            jnp.where(inner == first_width + 2, row_owner.astype(jnp.float32)[None, :], turned),
        ),
    ).astype(jnp.bfloat16)
    got_a = exchange(turned.reshape(owners, packed, row_total))
    turned_b = token_grad[:, first_span:].T.reshape(owners, second_width, row_total)
    turned_b, got_a = lax.optimization_barrier((turned_b, got_a))
    got_b = exchange(turned_b)

    keep, send = head_parts(hidden, dlogits, section, quarter)
    core = lax.ppermute(send, "section", CORE)
    onward = (keep[1].astype(jnp.float32) + core[1].astype(jnp.float32)).astype(jnp.bfloat16)
    far = lax.ppermute(onward, "section", ACROSS)

    got_a, onward = lax.optimization_barrier((got_a, onward))
    numbers = got_a[:, first_width : first_width + 3, :].astype(jnp.float32)
    ids = (numbers[:, 0] * 32.0 + numbers[:, 1] - 1.0).reshape(owners, blocks, BLOCK)
    owner = numbers[:, 2, ::BLOCK].astype(jnp.int32).reshape(-1)

    sums_a = owner_sums(got_a, owner, ids, slab_rows)
    back_a = exchange(sums_a)
    sums_b = owner_sums(got_b, owner, ids, slab_rows)
    back_b = exchange(sums_b)

    shares = (keep, core, far, master, moment1, moment2)
    *states, own_a = adam(back_a, first_width, 0, *shares)
    far_a = lax.ppermute(own_a, "section", ACROSS)
    core_a = lax.ppermute(own_a, "section", CORE)
    *states, own_b = adam(back_b, second_width, first_span, *shares, earlier=states)
    far_b = lax.ppermute(own_b, "section", ACROSS)
    core_b = lax.ppermute(own_b, "section", CORE)
    cross_a = lax.ppermute(far_a, "section", CORE)
    cross_b = lax.ppermute(far_b, "section", CORE)
    refreshed = assemble(
        section,
        ((own_a, own_b), (core_a, core_b), (far_a, far_b), (cross_a, cross_b)),
    )
    return (*states, refreshed)


def solution(mesh):
    placed = (
        P("vocab", "section"),
        P("vocab"),
        P("vocab", None),
        P("section", None),
        P("section", "vocab"),
        P("vocab", "section"),
        P("vocab", "section"),
        P("vocab", "section"),
    )
    return jax.shard_map(
        shards,
        mesh=mesh,
        in_specs=placed,
        out_specs=(
            P("vocab", "section"),
            P("vocab", "section"),
            P("vocab", "section"),
            P("vocab", None),
        ),
        check_vma=False,
    )
```

```python
import functools

import jax
import jax.numpy as jnp
from jax import lax
from jax.experimental import pallas as pl
from jax.experimental.pallas import tpu as pltpu
from jax.sharding import PartitionSpec as P

BLOCK = 128
MIB = 1024 * 1024


beta_first = 0.9
beta_second = 0.999
learn_rate = 0.01
adam_epsilon = 1e-08
first_fix = 1.0 - 0.9**10
second_fix = 1.0 - 0.999**10

CORE = ((0, 1), (1, 0), (2, 3), (3, 2))
ACROSS = ((0, 2), (2, 0), (1, 3), (3, 1))


def head_kernel(place, mine, theirs, hidden, hidden_theirs, own, early, late):
    half = pl.program_id(0)

    def product():
        return jnp.dot(mine[...], hidden[...], preferred_element_type=jnp.float32) + jnp.dot(
            theirs[...], hidden_theirs[...], preferred_element_type=jnp.float32
        )

    @pl.when(half == 0)
    def _():
        both = product().astype(jnp.bfloat16)
        early[...] = both[:, :512]
        late[...] = both[:, 512:]

    @pl.when(half == 1)
    def _():
        own[...] = product()


def head_parts(section, hidden, dlogits, hidden_theirs, dlogits_theirs):
    tokens, rows = dlogits.shape
    quarter = hidden.shape[1] // 4
    left = pl.BlockSpec((rows, tokens), lambda h, place: (0, 0))
    right = pl.BlockSpec((tokens, quarter), lambda h, place: (0, place[0] ^ (2 - 2 * h)))
    shapes = [
        jax.ShapeDtypeStruct((rows, quarter), jnp.float32),
        jax.ShapeDtypeStruct((rows, 512), jnp.bfloat16),
        jax.ShapeDtypeStruct((rows, quarter - 512), jnp.bfloat16),
    ]
    return pl.pallas_call(
        head_kernel,
        grid_spec=pltpu.PrefetchScalarGridSpec(
            num_scalar_prefetch=1,
            grid=(2,),
            in_specs=[left, left, right, right],
            out_specs=[pl.BlockSpec(shape.shape, lambda h, place: (0, 0)) for shape in shapes],
        ),
        out_shape=shapes,
        compiler_params=pltpu.CompilerParams(vmem_limit_bytes=58 * MIB),
        cost_estimate=pl.CostEstimate(
            flops=4 * tokens * rows * 2 * quarter,
            bytes_accessed=4 * tokens * (2 * quarter + rows) + 8 * rows * quarter,
            transcendentals=0,
        ),
    )(section.reshape(1), dlogits.T, dlogits_theirs.T, hidden, hidden_theirs)


SENDERS = 4


def sum_kernel(marks, got, out, acc, parts, ids, place, place_smem, sem):
    step = pl.program_id(0)
    members, _, slab_rows = acc.shape
    senders = got.shape[0]
    blocks = got.shape[2] // BLOCK

    @pl.when(step == 0)
    def _():
        lane = lax.broadcasted_iota(jnp.int32, (1, BLOCK), 1)
        for member in range(members):
            mark = marks[member].astype(jnp.float32)
            numbers = mark[4:5] * 32.0 + mark[5:6] - 1.0
            owner = mark[6:7].astype(jnp.int32)
            spots = jnp.zeros((1, BLOCK), jnp.int32)
            for block in range(blocks):
                lanes = slice(block * BLOCK, (block + 1) * BLOCK)
                ids[member, block : block + 1] = numbers[:, lanes]
                spots = jnp.where(lane == block, owner[:, lanes], spots)
            place[member : member + 1] = spots
        copy = pltpu.make_async_copy(place, place_smem, sem)
        copy.start()
        acc[...] = jnp.zeros_like(acc)
        copy.wait()

    lane = lax.broadcasted_iota(jnp.int32, (BLOCK, slab_rows), 1).astype(jnp.float32)

    def add(sender):
        for block in range(blocks):
            spot = place_smem[step * senders + sender, block]
            acc[spot] += parts[sender * blocks + block]

    for sender in range(senders):
        columns = ids[step * senders + sender].T
        for block in range(blocks):
            part = got[sender, :, block * BLOCK : (block + 1) * BLOCK]
            one_hot = (lane == columns[:, block : block + 1]).astype(jnp.bfloat16)
            parts[sender * blocks + block] = jnp.dot(
                part, one_hot, preferred_element_type=jnp.float32
            )
        if sender > 0:
            add(sender - 1)
    add(senders - 1)

    @pl.when(step == pl.num_programs(0) - 1)
    def _():
        def narrow(spot, carry):
            out[spot] = acc[spot].astype(jnp.bfloat16)
            return carry

        lax.fori_loop(0, members, narrow, 0)


def owner_sums(got, slab_rows):
    members, rows, row_total = got.shape
    blocks = row_total // BLOCK
    shape = (members, rows, slab_rows)
    return pl.pallas_call(
        sum_kernel,
        grid=(members // SENDERS,),
        in_specs=[
            pl.BlockSpec((members, 8, row_total), lambda i: (0, rows // 8 - 1, 0)),
            pl.BlockSpec((SENDERS, rows, row_total), lambda i: (i, 0, 0)),
        ],
        out_specs=pl.BlockSpec(shape, lambda i: (0, 0, 0)),
        out_shape=jax.ShapeDtypeStruct(shape, jnp.bfloat16),
        scratch_shapes=[
            pltpu.VMEM((members, rows, slab_rows), jnp.float32),
            pltpu.VMEM((SENDERS * blocks, rows, slab_rows), jnp.float32),
            pltpu.VMEM((members, blocks, BLOCK), jnp.float32),
            pltpu.VMEM((members, BLOCK), jnp.int32),
            pltpu.SMEM((members, BLOCK), jnp.int32),
            pltpu.SemaphoreType.DMA,
        ],
        compiler_params=pltpu.CompilerParams(vmem_limit_bytes=20 * MIB),
        cost_estimate=pl.CostEstimate(
            flops=2 * members * row_total * slab_rows * 400,
            bytes_accessed=2 * members * rows * (row_total + slab_rows),
            transcendentals=0,
        ),
    )(got, got)


def turned(block):
    size = block.shape[1]
    down = lax.broadcasted_iota(jnp.int32, (size, size), 0)
    unit = (down == lax.broadcasted_iota(jnp.int32, (size, size), 1)).astype(jnp.bfloat16)
    return lax.dot_general(
        unit, block, (((1,), (1,)), ((), ())), preferred_element_type=jnp.float32
    ).astype(jnp.bfloat16)


def message_kernel(counts, ids, first, second, third, out, rest, marks):
    step = pl.program_id(0)
    blocks = ids.shape[0]

    @pl.when(step == 0)
    def _():
        owners = counts.shape[1]
        shape = (owners, owners)
        before = lax.broadcasted_iota(jnp.int32, shape, 0) <= lax.broadcasted_iota(
            jnp.int32, shape, 1
        )
        ends = jnp.dot(
            jnp.broadcast_to(counts[...].astype(jnp.float32), (8, owners)).astype(jnp.bfloat16),
            before.astype(jnp.bfloat16),
            preferred_element_type=jnp.float32,
        )
        at = lax.broadcasted_iota(jnp.int32, ends.shape, 0).astype(jnp.float32)
        owner = jnp.sum((ends <= at).astype(jnp.float32), axis=1, keepdims=True)
        owner = jnp.broadcast_to(owner, ids.shape)
        shifted = ids[...] + 1
        high = (shifted >> 5).astype(jnp.float32)
        low = (shifted & 31).astype(jnp.float32)
        marks[...] = jnp.zeros_like(marks)
        for block in range(blocks):
            lanes = slice(block * BLOCK, (block + 1) * BLOCK)
            row = slice(block, block + 1)
            marks[0:1, lanes] = high[row]
            marks[1:2, lanes] = low[row]
            marks[2:3, lanes] = owner[row]
        tail = turned(third[...]).astype(jnp.float32)
        for member in range(rest.shape[0]):
            both = jnp.concatenate([tail[member * 4 : member * 4 + 4], marks[0:4]], axis=0)
            rest[member] = both.astype(jnp.bfloat16)

    a = turned(first[...])
    b = turned(second[...])
    for member in range(8):
        out[member, :16] = a[member * 16 : member * 16 + 16]
        out[member, 16:32] = b[member * 16 : member * 16 + 16]
        out[member, 32:] = rest[step * 8 + member]


def messages(block_counts, token_ids, token_grad):
    row_total = token_grad.shape[0]
    blocks = row_total // BLOCK
    return pl.pallas_call(
        message_kernel,
        grid=(4,),
        in_specs=[
            pl.BlockSpec(block_counts.shape, lambda i: (0, 0)),
            pl.BlockSpec((blocks, BLOCK), lambda i: (0, 0)),
            pl.BlockSpec((row_total, 128), lambda i: (0, i)),
            pl.BlockSpec((row_total, 128), lambda i: (0, 4 + i)),
            pl.BlockSpec((row_total, 128), lambda i: (0, 8)),
        ],
        out_specs=pl.BlockSpec((8, 40, row_total), lambda i: (i, 0, 0)),
        out_shape=jax.ShapeDtypeStruct((32, 40, row_total), jnp.bfloat16),
        scratch_shapes=[
            pltpu.VMEM((32, 8, row_total), jnp.bfloat16),
            pltpu.VMEM((8, row_total), jnp.float32),
        ],
        compiler_params=pltpu.CompilerParams(vmem_limit_bytes=58 * MIB),
        cost_estimate=pl.CostEstimate(
            flops=2 * row_total * 1152 * 128,
            bytes_accessed=2 * row_total * (1152 + 1280),
            transcendentals=0,
        ),
    )(block_counts, token_ids.reshape(blocks, BLOCK), token_grad, token_grad, token_grad)


def adam_kernel(tail, back, rest, head, far, master, moment1, moment2, *more):
    out_master, out_moment1, out_moment2, out_own, unit, total = more[-6:]
    step = pl.program_id(0)
    _, _, slab_rows = back.shape
    lanes = out_own.shape[1]

    @pl.when(step == 0)
    def _():
        down = lax.broadcasted_iota(jnp.int32, unit.shape, 0)
        unit[...] = (down == lax.broadcasted_iota(jnp.int32, unit.shape, 1)).astype(jnp.bfloat16)

    def upright(part):
        return lax.dot_general(
            unit[...], part, (((1,), (1,)), ((), ())), preferred_element_type=jnp.float32
        )

    if tail:

        @pl.when(step < 4)
        def _():
            total[...] = upright(back[...].reshape(lanes, slab_rows))

        @pl.when(step == 4)
        def _():
            shape = (lanes, 2 * lanes)
            feature = lax.broadcasted_iota(jnp.int32, shape, 0)
            line = lax.broadcasted_iota(jnp.int32, shape, 1)
            select = jnp.logical_and((line // 8) * 4 + line % 8 == feature, line % 8 < 4)
            part = jnp.dot(
                select.astype(jnp.bfloat16),
                rest[...].reshape(2 * lanes, slab_rows),
                preferred_element_type=jnp.float32,
            )
            total[...] = upright(part.astype(jnp.bfloat16))
    else:
        total[...] = upright(back[...].reshape(lanes, slab_rows))

    gradient = total[...] + head[...] + far[...].astype(jnp.float32)
    first = beta_first * moment1[...] + (1.0 - beta_first) * gradient
    second = beta_second * moment2[...] + (1.0 - beta_second) * gradient * gradient
    fresh = master[...] - (learn_rate / first_fix) * first / (
        jnp.sqrt(second * (1.0 / second_fix)) + adam_epsilon
    )
    out_master[...] = fresh
    out_moment1[...] = first
    out_moment2[...] = second
    out_own[...] = fresh.astype(jnp.bfloat16)


def adam(back, group, span, head, far, master, moment1, moment2, earlier=()):
    members, rows, slab_rows = back.shape
    lanes = 128
    first = 4 * group
    tile = pl.BlockSpec((slab_rows, lanes), lambda i: (0, first + i))
    whole = jax.ShapeDtypeStruct(master.shape, jnp.float32)
    return pl.pallas_call(
        functools.partial(adam_kernel, span > 512),
        grid=(span // lanes,),
        in_specs=[
            pl.BlockSpec((8, 16, slab_rows), lambda i: (jnp.minimum(i, 3), group, 0)),
            pl.BlockSpec((members, 8, slab_rows), lambda i: (0, rows // 8 - 1, 0)),
            tile,
            pl.BlockSpec((slab_rows, lanes), lambda i: (0, i)),
            tile,
            tile,
            tile,
        ]
        + [pl.BlockSpec(memory_space=pl.ANY)] * len(earlier),
        out_specs=[tile, tile, tile, pl.BlockSpec((slab_rows, lanes), lambda i: (0, i))],
        out_shape=[whole, whole, whole, jax.ShapeDtypeStruct((slab_rows, span), jnp.bfloat16)],
        scratch_shapes=[
            pltpu.VMEM((slab_rows, slab_rows), jnp.bfloat16),
            pltpu.VMEM((slab_rows, lanes), jnp.float32),
        ],
        input_output_aliases={7 + at: at for at in range(len(earlier))},
        compiler_params=pltpu.CompilerParams(vmem_limit_bytes=58 * MIB),
        cost_estimate=pl.CostEstimate(
            flops=4 * lanes * span * slab_rows,
            bytes_accessed=slab_rows * span * 36,
            transcendentals=slab_rows * span,
        ),
    )(back, back, head, far, master, moment1, moment2, *earlier)


def place_kernel(count, place, *refs):
    parts, out = refs[:-1], refs[-1]
    quarter = out.shape[1] // 4
    for k in range(4):
        start = (place[0] ^ k) * quarter
        for at in range(count):
            part = parts[k * count + at]
            size = part.shape[1]
            out[:, pl.ds(pl.multiple_of(start, 128), size)] = part[...]
            start = start + size


def assemble(section, pieces):
    count = len(pieces[0])
    rows = pieces[0][0].shape[0]
    quarter = sum(part.shape[1] for part in pieces[0])
    some = 176
    parts = [part for piece in pieces for part in piece]
    return pl.pallas_call(
        functools.partial(place_kernel, count),
        grid_spec=pltpu.PrefetchScalarGridSpec(
            num_scalar_prefetch=1,
            grid=(-(-rows // some),),
            in_specs=[pl.BlockSpec((some, part.shape[1]), lambda i, place: (i, 0)) for part in parts],
            out_specs=pl.BlockSpec((some, 4 * quarter), lambda i, place: (i, 0)),
        ),
        out_shape=jax.ShapeDtypeStruct((rows, 4 * quarter), jnp.bfloat16),
        compiler_params=pltpu.CompilerParams(vmem_limit_bytes=20 * MIB),
        cost_estimate=pl.CostEstimate(
            flops=0, bytes_accessed=4 * rows * quarter * 4, transcendentals=0
        ),
    )(section.reshape(1), *parts)


def exchange(rows):
    return lax.all_to_all(rows, "vocab", split_axis=0, concat_axis=0, tiled=True)


def shards(token_grad, token_ids, block_counts, hidden, dlogits, master, moment1, moment2):
    section = lax.axis_index("section").astype(jnp.int32)
    quarter = token_grad.shape[1]
    slab_rows = master.shape[0]
    hidden_theirs = lax.ppermute(hidden, "section", CORE)
    dlogits_theirs = lax.ppermute(dlogits, "section", CORE)
    got = exchange(messages(block_counts, token_ids, token_grad))

    head, early, late = head_parts(section, hidden, dlogits, hidden_theirs, dlogits_theirs)
    got, early, late = lax.optimization_barrier((got, early, late))
    early = lax.ppermute(early, "section", ACROSS)
    late = lax.ppermute(late, "section", ACROSS)
    sums, early = lax.optimization_barrier((owner_sums(got, slab_rows), early))
    back = exchange(sums)

    states = (master, moment1, moment2)
    *states, own_a = adam(back, 0, 512, head, early, *states)
    far_a = lax.ppermute(own_a, "section", ACROSS)
    core_a = lax.ppermute(own_a, "section", CORE)
    *states, own_b = adam(
        back, 1, quarter - 512, head, late, master, moment1, moment2, earlier=states
    )
    turn_b, far_a = lax.optimization_barrier((own_b, far_a))
    far_b = lax.ppermute(turn_b, "section", ACROSS)
    core_b = lax.ppermute(own_b, "section", CORE)
    cross_a = lax.ppermute(far_a, "section", CORE)
    cross_b = lax.ppermute(far_b, "section", CORE)
    refreshed = assemble(
        section,
        ((own_a, own_b), (core_a, core_b), (far_a, far_b), (cross_a, cross_b)),
    )
    return (*states, refreshed)


def solution(mesh):
    placed = (
        P("vocab", "section"),
        P("vocab"),
        P("vocab", None),
        P("section", None),
        P("section", "vocab"),
        P("vocab", "section"),
        P("vocab", "section"),
        P("vocab", "section"),
    )
    return jax.shard_map(
        shards,
        mesh=mesh,
        in_specs=placed,
        out_specs=(
            P("vocab", "section"),
            P("vocab", "section"),
            P("vocab", "section"),
            P("vocab", None),
        ),
        check_vma=False,
    )
```

```python
import functools

import jax
import jax.numpy as jnp
from jax import lax
from jax.experimental import pallas as pl
from jax.experimental.pallas import tpu as pltpu
from jax.sharding import PartitionSpec as P

BLOCK = 128
MIB = 1024 * 1024


beta_first = 0.9
beta_second = 0.999
learn_rate = 0.01
adam_epsilon = 1e-08
first_fix = 1.0 - 0.9**10
second_fix = 1.0 - 0.999**10

CORE = ((0, 1), (1, 0), (2, 3), (3, 2))
ACROSS = ((0, 2), (2, 0), (1, 3), (3, 1))


def head_kernel(place, mine, theirs, hidden, hidden_theirs, own, early, late):
    half = pl.program_id(0)

    def product():
        return jnp.dot(mine[...], hidden[...], preferred_element_type=jnp.float32) + jnp.dot(
            theirs[...], hidden_theirs[...], preferred_element_type=jnp.float32
        )

    @pl.when(half == 0)
    def _():
        both = product().astype(jnp.bfloat16)
        early[...] = both[:, :640]
        late[...] = both[:, 640:]

    @pl.when(half == 1)
    def _():
        own[...] = product().astype(jnp.bfloat16)


def head_parts(section, hidden, dlogits, hidden_theirs, dlogits_theirs):
    tokens, rows = dlogits.shape
    quarter = hidden.shape[1] // 4
    left = pl.BlockSpec((rows, tokens), lambda h, place: (0, 0))
    right = pl.BlockSpec((tokens, quarter), lambda h, place: (0, place[0] ^ (2 - 2 * h)))
    shapes = [
        jax.ShapeDtypeStruct((rows, quarter), jnp.bfloat16),
        jax.ShapeDtypeStruct((rows, 640), jnp.bfloat16),
        jax.ShapeDtypeStruct((rows, quarter - 640), jnp.bfloat16),
    ]
    return pl.pallas_call(
        head_kernel,
        grid_spec=pltpu.PrefetchScalarGridSpec(
            num_scalar_prefetch=1,
            grid=(2,),
            in_specs=[left, left, right, right],
            out_specs=[pl.BlockSpec(shape.shape, lambda h, place: (0, 0)) for shape in shapes],
        ),
        out_shape=shapes,
        compiler_params=pltpu.CompilerParams(vmem_limit_bytes=58 * MIB),
        cost_estimate=pl.CostEstimate(
            flops=4 * tokens * rows * 2 * quarter,
            bytes_accessed=4 * tokens * (2 * quarter + rows) + 8 * rows * quarter,
            transcendentals=0,
        ),
    )(section.reshape(1), dlogits.T, dlogits_theirs.T, hidden, hidden_theirs)


SENDERS = 4


def sum_kernel(marks, got, out, acc, parts, ids, place, place_smem, sem):
    step = pl.program_id(0)
    members, _, slab_rows = acc.shape
    senders = got.shape[0]
    blocks = got.shape[2] // BLOCK

    @pl.when(step == 0)
    def _():
        lane = lax.broadcasted_iota(jnp.int32, (1, BLOCK), 1)
        for member in range(members):
            mark = marks[member].astype(jnp.float32)
            numbers = mark[4:5] * 32.0 + mark[5:6] - 1.0
            owner = mark[6:7].astype(jnp.int32)
            spots = jnp.zeros((1, BLOCK), jnp.int32)
            for block in range(blocks):
                lanes = slice(block * BLOCK, (block + 1) * BLOCK)
                ids[member, block : block + 1] = numbers[:, lanes]
                spots = jnp.where(lane == block, owner[:, lanes], spots)
            place[member : member + 1] = spots
        copy = pltpu.make_async_copy(place, place_smem, sem)
        copy.start()
        acc[...] = jnp.zeros_like(acc)
        copy.wait()

    lane = lax.broadcasted_iota(jnp.int32, (BLOCK, slab_rows), 1).astype(jnp.float32)

    def add(sender):
        for block in range(blocks):
            spot = place_smem[step * senders + sender, block]
            acc[spot] += parts[sender * blocks + block]

    for sender in range(senders):
        columns = ids[step * senders + sender].T
        for block in range(blocks):
            part = got[sender, :, block * BLOCK : (block + 1) * BLOCK]
            one_hot = (lane == columns[:, block : block + 1]).astype(jnp.bfloat16)
            parts[sender * blocks + block] = jnp.dot(
                part, one_hot, preferred_element_type=jnp.float32
            )
        if sender > 0:
            add(sender - 1)
    add(senders - 1)

    @pl.when(step == pl.num_programs(0) - 1)
    def _():
        def narrow(spot, carry):
            out[spot] = acc[spot].astype(jnp.bfloat16)
            return carry

        lax.fori_loop(0, members, narrow, 0)


def owner_sums(got, slab_rows):
    members, rows, row_total = got.shape
    blocks = row_total // BLOCK
    shape = (members, rows, slab_rows)
    return pl.pallas_call(
        sum_kernel,
        grid=(members // SENDERS,),
        in_specs=[
            pl.BlockSpec((members, 8, row_total), lambda i: (0, rows // 8 - 1, 0)),
            pl.BlockSpec((SENDERS, rows, row_total), lambda i: (i, 0, 0)),
        ],
        out_specs=pl.BlockSpec(shape, lambda i: (0, 0, 0)),
        out_shape=jax.ShapeDtypeStruct(shape, jnp.bfloat16),
        scratch_shapes=[
            pltpu.VMEM((members, rows, slab_rows), jnp.float32),
            pltpu.VMEM((SENDERS * blocks, rows, slab_rows), jnp.float32),
            pltpu.VMEM((members, blocks, BLOCK), jnp.float32),
            pltpu.VMEM((members, BLOCK), jnp.int32),
            pltpu.SMEM((members, BLOCK), jnp.int32),
            pltpu.SemaphoreType.DMA,
        ],
        compiler_params=pltpu.CompilerParams(vmem_limit_bytes=20 * MIB),
        cost_estimate=pl.CostEstimate(
            flops=2 * members * row_total * slab_rows * 400,
            bytes_accessed=2 * members * rows * (row_total + slab_rows),
            transcendentals=0,
        ),
    )(got, got)


def turned(block):
    size = block.shape[1]
    down = lax.broadcasted_iota(jnp.int32, (size, size), 0)
    unit = (down == lax.broadcasted_iota(jnp.int32, (size, size), 1)).astype(jnp.bfloat16)
    return lax.dot_general(
        unit, block, (((1,), (1,)), ((), ())), preferred_element_type=jnp.float32
    ).astype(jnp.bfloat16)


def message_kernel(counts, ids, first, second, third, out, rest, marks):
    step = pl.program_id(0)
    blocks = ids.shape[0]

    @pl.when(step == 0)
    def _():
        owners = counts.shape[1]
        shape = (owners, owners)
        before = lax.broadcasted_iota(jnp.int32, shape, 0) <= lax.broadcasted_iota(
            jnp.int32, shape, 1
        )
        ends = jnp.dot(
            jnp.broadcast_to(counts[...].astype(jnp.float32), (8, owners)).astype(jnp.bfloat16),
            before.astype(jnp.bfloat16),
            preferred_element_type=jnp.float32,
        )
        at = lax.broadcasted_iota(jnp.int32, ends.shape, 0).astype(jnp.float32)
        owner = jnp.sum((ends <= at).astype(jnp.float32), axis=1, keepdims=True)
        owner = jnp.broadcast_to(owner, ids.shape)
        shifted = ids[...] + 1
        high = (shifted >> 5).astype(jnp.float32)
        low = (shifted & 31).astype(jnp.float32)
        marks[...] = jnp.zeros_like(marks)
        for block in range(blocks):
            lanes = slice(block * BLOCK, (block + 1) * BLOCK)
            row = slice(block, block + 1)
            marks[0:1, lanes] = high[row]
            marks[1:2, lanes] = low[row]
            marks[2:3, lanes] = owner[row]
        tail = turned(third[...]).astype(jnp.float32)
        for member in range(rest.shape[0]):
            both = jnp.concatenate([tail[member * 4 : member * 4 + 4], marks[0:4]], axis=0)
            rest[member] = both.astype(jnp.bfloat16)

    a = turned(first[...])
    b = turned(second[...])
    for member in range(8):
        out[member, :16] = a[member * 16 : member * 16 + 16]
        out[member, 16:32] = b[member * 16 : member * 16 + 16]
        out[member, 32:] = rest[step * 8 + member]


def messages(block_counts, token_ids, token_grad):
    row_total = token_grad.shape[0]
    blocks = row_total // BLOCK
    return pl.pallas_call(
        message_kernel,
        grid=(4,),
        in_specs=[
            pl.BlockSpec(block_counts.shape, lambda i: (0, 0)),
            pl.BlockSpec((blocks, BLOCK), lambda i: (0, 0)),
            pl.BlockSpec((row_total, 128), lambda i: (0, i)),
            pl.BlockSpec((row_total, 128), lambda i: (0, 4 + i)),
            pl.BlockSpec((row_total, 128), lambda i: (0, 8)),
        ],
        out_specs=pl.BlockSpec((8, 40, row_total), lambda i: (i, 0, 0)),
        out_shape=jax.ShapeDtypeStruct((32, 40, row_total), jnp.bfloat16),
        scratch_shapes=[
            pltpu.VMEM((32, 8, row_total), jnp.bfloat16),
            pltpu.VMEM((8, row_total), jnp.float32),
        ],
        compiler_params=pltpu.CompilerParams(vmem_limit_bytes=58 * MIB),
        cost_estimate=pl.CostEstimate(
            flops=2 * row_total * 1152 * 128,
            bytes_accessed=2 * row_total * (1152 + 1280),
            transcendentals=0,
        ),
    )(block_counts, token_ids.reshape(blocks, BLOCK), token_grad, token_grad, token_grad)


def adam_kernel(early, tail, back, rest, head, *more):
    far, (master, moment1, moment2) = more[: len(early)], more[len(early) : len(early) + 3]
    out_master, out_moment1, out_moment2, out_own, unit, total = more[-6:]
    step = pl.program_id(0)
    slab_rows, lanes = out_own.shape

    @pl.when(step == 0)
    def _():
        down = lax.broadcasted_iota(jnp.int32, unit.shape, 0)
        unit[...] = (down == lax.broadcasted_iota(jnp.int32, unit.shape, 1)).astype(jnp.bfloat16)

    def upright(part):
        return lax.dot_general(
            unit[...], part, (((1,), (1,)), ((), ())), preferred_element_type=jnp.float32
        )

    if tail:

        @pl.when(step < 4)
        def _():
            total[...] = upright(back[...].reshape(lanes, slab_rows))

        @pl.when(step == 4)
        def _():
            shape = (lanes, 2 * lanes)
            feature = lax.broadcasted_iota(jnp.int32, shape, 0)
            line = lax.broadcasted_iota(jnp.int32, shape, 1)
            select = jnp.logical_and((line // 8) * 4 + line % 8 == feature, line % 8 < 4)
            part = jnp.dot(
                select.astype(jnp.bfloat16),
                rest[...].reshape(2 * lanes, slab_rows),
                preferred_element_type=jnp.float32,
            )
            total[...] = upright(part.astype(jnp.bfloat16))
    else:
        total[...] = upright(back[...].reshape(lanes, slab_rows))

    from_far = far[0][...].astype(jnp.float32)
    if len(early) == 2:
        from_far = jnp.where(step < early[1], from_far, far[1][...].astype(jnp.float32))
    gradient = total[...] + head[...].astype(jnp.float32) + from_far
    first = beta_first * moment1[...] + (1.0 - beta_first) * gradient
    second = beta_second * moment2[...] + (1.0 - beta_second) * gradient * gradient
    fresh = master[...] - (learn_rate / first_fix) * first / (
        jnp.sqrt(second * (1.0 / second_fix)) + adam_epsilon
    )
    out_master[...] = fresh
    out_moment1[...] = first
    out_moment2[...] = second
    out_own[...] = fresh.astype(jnp.bfloat16)


def adam(back, group, lanes, head, far, master, moment1, moment2, earlier=()):
    members, rows, slab_rows = back.shape
    quarter = master.shape[1]
    span = 512 if group == 0 else quarter - 512
    first = 512 * group // lanes
    tile = pl.BlockSpec((slab_rows, lanes), lambda i: (0, first + i))

    def far_spec(begin, array):
        last = array.shape[1] // lanes - 1
        return pl.BlockSpec((slab_rows, lanes), lambda i: (0, jnp.clip(first + i - begin, 0, last)))

    begins = [0, far[0].shape[1] // lanes][: len(far)]
    whole = jax.ShapeDtypeStruct(master.shape, jnp.float32)
    return pl.pallas_call(
        functools.partial(adam_kernel, [begin - first for begin in begins], span > 512),
        grid=(span // lanes,),
        in_specs=[
            pl.BlockSpec(
                (lanes // 16, 16, slab_rows), lambda i: (jnp.minimum(i, 512 // lanes - 1), group, 0)
            ),
            pl.BlockSpec((members, 8, slab_rows), lambda i: (0, rows // 8 - 1, 0)),
            tile,
            *[far_spec(*pair) for pair in zip(begins, far)],
            tile,
            tile,
            tile,
        ]
        + [pl.BlockSpec(memory_space=pl.ANY)] * len(earlier),
        out_specs=[tile, tile, tile, pl.BlockSpec((slab_rows, lanes), lambda i: (0, i))],
        out_shape=[whole, whole, whole, jax.ShapeDtypeStruct((slab_rows, span), jnp.bfloat16)],
        scratch_shapes=[
            pltpu.VMEM((slab_rows, slab_rows), jnp.bfloat16),
            pltpu.VMEM((slab_rows, lanes), jnp.float32),
        ],
        input_output_aliases={6 + len(far) + at: at for at in range(len(earlier))},
        compiler_params=pltpu.CompilerParams(vmem_limit_bytes=52 * MIB),
        cost_estimate=pl.CostEstimate(
            flops=4 * 128 * span * slab_rows,
            bytes_accessed=slab_rows * span * 36,
            transcendentals=slab_rows * span,
        ),
    )(back, back, head, *far, master, moment1, moment2, *earlier)


def place_kernel(count, place, *refs):
    parts, out = refs[:-1], refs[-1]
    quarter = out.shape[1] // 4
    for k in range(4):
        start = (place[0] ^ k) * quarter
        for at in range(count):
            part = parts[k * count + at]
            size = part.shape[1]
            out[:, pl.ds(pl.multiple_of(start, 128), size)] = part[...]
            start = start + size


def assemble(section, pieces):
    count = len(pieces[0])
    rows = pieces[0][0].shape[0]
    quarter = sum(part.shape[1] for part in pieces[0])
    some = 176
    parts = [part for piece in pieces for part in piece]
    return pl.pallas_call(
        functools.partial(place_kernel, count),
        grid_spec=pltpu.PrefetchScalarGridSpec(
            num_scalar_prefetch=1,
            grid=(-(-rows // some),),
            in_specs=[pl.BlockSpec((some, part.shape[1]), lambda i, place: (i, 0)) for part in parts],
            out_specs=pl.BlockSpec((some, 4 * quarter), lambda i, place: (i, 0)),
        ),
        out_shape=jax.ShapeDtypeStruct((rows, 4 * quarter), jnp.bfloat16),
        compiler_params=pltpu.CompilerParams(vmem_limit_bytes=20 * MIB),
        cost_estimate=pl.CostEstimate(
            flops=0, bytes_accessed=4 * rows * quarter * 4, transcendentals=0
        ),
    )(section.reshape(1), *parts)


def exchange(rows):
    return lax.all_to_all(rows, "vocab", split_axis=0, concat_axis=0, tiled=True)


def shards(token_grad, token_ids, block_counts, hidden, dlogits, master, moment1, moment2):
    section = lax.axis_index("section").astype(jnp.int32)
    quarter = token_grad.shape[1]
    slab_rows = master.shape[0]
    hidden_theirs = lax.ppermute(hidden, "section", CORE)
    dlogits_theirs = lax.ppermute(dlogits, "section", CORE)
    got = exchange(messages(block_counts, token_ids, token_grad))

    head, early, late = head_parts(section, hidden, dlogits, hidden_theirs, dlogits_theirs)
    got, early, late = lax.optimization_barrier((got, early, late))
    early = lax.ppermute(early, "section", ACROSS)
    late = lax.ppermute(late, "section", ACROSS)
    sums, early = lax.optimization_barrier((owner_sums(got, slab_rows), early))
    back = exchange(sums)

    *states, own_a = adam(back, 0, 256, head, [early], master, moment1, moment2)
    far_a = lax.ppermute(own_a, "section", ACROSS)
    core_a = lax.ppermute(own_a, "section", CORE)
    *states, own_b = adam(
        back, 1, 128, head, [early, late], master, moment1, moment2, earlier=states
    )
    turn_b, far_a = lax.optimization_barrier((own_b, far_a))
    far_b = lax.ppermute(turn_b, "section", ACROSS)
    core_b = lax.ppermute(own_b, "section", CORE)
    cross_a = lax.ppermute(far_a, "section", CORE)
    cross_b = lax.ppermute(far_b, "section", CORE)
    refreshed = assemble(
        section,
        ((own_a, own_b), (core_a, core_b), (far_a, far_b), (cross_a, cross_b)),
    )
    return (*states, refreshed)


def solution(mesh):
    placed = (
        P("vocab", "section"),
        P("vocab"),
        P("vocab", None),
        P("section", None),
        P("section", "vocab"),
        P("vocab", "section"),
        P("vocab", "section"),
        P("vocab", "section"),
    )
    return jax.shard_map(
        shards,
        mesh=mesh,
        in_specs=placed,
        out_specs=(
            P("vocab", "section"),
            P("vocab", "section"),
            P("vocab", "section"),
            P("vocab", None),
        ),
        check_vma=False,
    )
```

```python
import functools

import jax
import jax.numpy as jnp
from jax import lax
from jax.experimental import pallas as pl
from jax.experimental.pallas import tpu as pltpu
from jax.sharding import PartitionSpec as P

BLOCK = 128
MIB = 1024 * 1024


beta_first = 0.9
beta_second = 0.999
learn_rate = 0.01
adam_epsilon = 1e-08
first_fix = 1.0 - 0.9**10
second_fix = 1.0 - 0.999**10

CORE = ((0, 1), (1, 0), (2, 3), (3, 2))
ACROSS = ((0, 2), (2, 0), (1, 3), (3, 1))


def head_kernel(place, mine, theirs, hidden, hidden_theirs, own, early, late):
    half = pl.program_id(0)

    def product():
        return jnp.dot(mine[...], hidden[...], preferred_element_type=jnp.float32) + jnp.dot(
            theirs[...], hidden_theirs[...], preferred_element_type=jnp.float32
        )

    @pl.when(half == 0)
    def _():
        both = product().astype(jnp.bfloat16)
        early[...] = both[:, :640]
        late[...] = both[:, 640:]

    @pl.when(half == 1)
    def _():
        own[...] = product().astype(jnp.bfloat16)


def head_parts(section, hidden, dlogits, hidden_theirs, dlogits_theirs):
    tokens, rows = dlogits.shape
    quarter = hidden.shape[1] // 4
    left = pl.BlockSpec((rows, tokens), lambda h, place: (0, 0))
    right = pl.BlockSpec((tokens, quarter), lambda h, place: (0, place[0] ^ (2 - 2 * h)))
    shapes = [
        jax.ShapeDtypeStruct((rows, quarter), jnp.bfloat16),
        jax.ShapeDtypeStruct((rows, 640), jnp.bfloat16),
        jax.ShapeDtypeStruct((rows, quarter - 640), jnp.bfloat16),
    ]
    return pl.pallas_call(
        head_kernel,
        grid_spec=pltpu.PrefetchScalarGridSpec(
            num_scalar_prefetch=1,
            grid=(2,),
            in_specs=[left, left, right, right],
            out_specs=[pl.BlockSpec(shape.shape, lambda h, place: (0, 0)) for shape in shapes],
        ),
        out_shape=shapes,
        compiler_params=pltpu.CompilerParams(vmem_limit_bytes=58 * MIB),
        cost_estimate=pl.CostEstimate(
            flops=4 * tokens * rows * 2 * quarter,
            bytes_accessed=4 * tokens * (2 * quarter + rows) + 8 * rows * quarter,
            transcendentals=0,
        ),
    )(section.reshape(1), dlogits.T, dlogits_theirs.T, hidden, hidden_theirs)


SENDERS = 4


def sum_kernel(marks, got, out, acc, parts, ids, place, place_smem, sem):
    step = pl.program_id(0)
    members, _, slab_rows = acc.shape
    senders = got.shape[0]
    blocks = got.shape[2] // BLOCK

    @pl.when(step == 0)
    def _():
        lane = lax.broadcasted_iota(jnp.int32, (1, BLOCK), 1)
        for member in range(members):
            mark = marks[member].astype(jnp.float32)
            numbers = mark[4:5] * 32.0 + mark[5:6] - 1.0
            owner = mark[6:7].astype(jnp.int32)
            spots = jnp.zeros((1, BLOCK), jnp.int32)
            for block in range(blocks):
                lanes = slice(block * BLOCK, (block + 1) * BLOCK)
                ids[member, block : block + 1] = numbers[:, lanes]
                spots = jnp.where(lane == block, owner[:, lanes], spots)
            place[member : member + 1] = spots
        copy = pltpu.make_async_copy(place, place_smem, sem)
        copy.start()
        acc[...] = jnp.zeros_like(acc)
        copy.wait()

    lane = lax.broadcasted_iota(jnp.int32, (BLOCK, slab_rows), 1).astype(jnp.float32)

    def add(sender):
        for block in range(blocks):
            spot = place_smem[step * senders + sender, block]
            acc[spot] += parts[sender * blocks + block]

    for sender in range(senders):
        columns = ids[step * senders + sender].T
        for block in range(blocks):
            part = got[sender, :, block * BLOCK : (block + 1) * BLOCK]
            one_hot = (lane == columns[:, block : block + 1]).astype(jnp.bfloat16)
            parts[sender * blocks + block] = jnp.dot(
                part, one_hot, preferred_element_type=jnp.float32
            )
        if sender > 0:
            add(sender - 1)
    add(senders - 1)

    @pl.when(step == pl.num_programs(0) - 1)
    def _():
        def narrow(spot, carry):
            out[spot] = acc[spot].astype(jnp.bfloat16)
            return carry

        lax.fori_loop(0, members, narrow, 0)


def owner_sums(got, slab_rows):
    members, rows, row_total = got.shape
    blocks = row_total // BLOCK
    shape = (members, rows, slab_rows)
    return pl.pallas_call(
        sum_kernel,
        grid=(members // SENDERS,),
        in_specs=[
            pl.BlockSpec((members, 8, row_total), lambda i: (0, rows // 8 - 1, 0)),
            pl.BlockSpec((SENDERS, rows, row_total), lambda i: (i, 0, 0)),
        ],
        out_specs=pl.BlockSpec(shape, lambda i: (0, 0, 0)),
        out_shape=jax.ShapeDtypeStruct(shape, jnp.bfloat16),
        scratch_shapes=[
            pltpu.VMEM((members, rows, slab_rows), jnp.float32),
            pltpu.VMEM((SENDERS * blocks, rows, slab_rows), jnp.float32),
            pltpu.VMEM((members, blocks, BLOCK), jnp.float32),
            pltpu.VMEM((members, BLOCK), jnp.int32),
            pltpu.SMEM((members, BLOCK), jnp.int32),
            pltpu.SemaphoreType.DMA,
        ],
        compiler_params=pltpu.CompilerParams(vmem_limit_bytes=20 * MIB),
        cost_estimate=pl.CostEstimate(flops=0, bytes_accessed=0, transcendentals=0),
    )(got, got)


def turned(block):
    size = block.shape[1]
    down = lax.broadcasted_iota(jnp.int32, (size, size), 0)
    unit = (down == lax.broadcasted_iota(jnp.int32, (size, size), 1)).astype(jnp.bfloat16)
    return lax.dot_general(
        unit, block, (((1,), (1,)), ((), ())), preferred_element_type=jnp.float32
    ).astype(jnp.bfloat16)


def message_kernel(counts, ids, first, second, third, out, rest, marks):
    step = pl.program_id(0)
    blocks = ids.shape[0]

    @pl.when(step == 0)
    def _():
        owners = counts.shape[1]
        shape = (owners, owners)
        before = lax.broadcasted_iota(jnp.int32, shape, 0) <= lax.broadcasted_iota(
            jnp.int32, shape, 1
        )
        ends = jnp.dot(
            jnp.broadcast_to(counts[...].astype(jnp.float32), (8, owners)).astype(jnp.bfloat16),
            before.astype(jnp.bfloat16),
            preferred_element_type=jnp.float32,
        )
        at = lax.broadcasted_iota(jnp.int32, ends.shape, 0).astype(jnp.float32)
        owner = jnp.sum((ends <= at).astype(jnp.float32), axis=1, keepdims=True)
        owner = jnp.broadcast_to(owner, ids.shape)
        shifted = ids[...] + 1
        high = (shifted >> 5).astype(jnp.float32)
        low = (shifted & 31).astype(jnp.float32)
        marks[...] = jnp.zeros_like(marks)
        for block in range(blocks):
            lanes = slice(block * BLOCK, (block + 1) * BLOCK)
            row = slice(block, block + 1)
            marks[0:1, lanes] = high[row]
            marks[1:2, lanes] = low[row]
            marks[2:3, lanes] = owner[row]
        tail = turned(third[...]).astype(jnp.float32)
        for member in range(rest.shape[0]):
            both = jnp.concatenate([tail[member * 4 : member * 4 + 4], marks[0:4]], axis=0)
            rest[member] = both.astype(jnp.bfloat16)

    a = turned(first[...])
    b = turned(second[...])
    for member in range(8):
        out[member, :16] = a[member * 16 : member * 16 + 16]
        out[member, 16:32] = b[member * 16 : member * 16 + 16]
        out[member, 32:] = rest[step * 8 + member]


def messages(block_counts, token_ids, token_grad):
    row_total = token_grad.shape[0]
    blocks = row_total // BLOCK
    return pl.pallas_call(
        message_kernel,
        grid=(4,),
        in_specs=[
            pl.BlockSpec(block_counts.shape, lambda i: (0, 0)),
            pl.BlockSpec((blocks, BLOCK), lambda i: (0, 0)),
            pl.BlockSpec((row_total, 128), lambda i: (0, i)),
            pl.BlockSpec((row_total, 128), lambda i: (0, 4 + i)),
            pl.BlockSpec((row_total, 128), lambda i: (0, 8)),
        ],
        out_specs=pl.BlockSpec((8, 40, row_total), lambda i: (i, 0, 0)),
        out_shape=jax.ShapeDtypeStruct((32, 40, row_total), jnp.bfloat16),
        scratch_shapes=[
            pltpu.VMEM((32, 8, row_total), jnp.bfloat16),
            pltpu.VMEM((8, row_total), jnp.float32),
        ],
        compiler_params=pltpu.CompilerParams(vmem_limit_bytes=58 * MIB),
        cost_estimate=pl.CostEstimate(
            flops=2 * row_total * 1152 * 128,
            bytes_accessed=2 * row_total * (1152 + 1280),
            transcendentals=0,
        ),
    )(block_counts, token_ids.reshape(blocks, BLOCK), token_grad, token_grad, token_grad)


def adam_kernel(early, tail, back, rest, head, *more):
    far, (master, moment1, moment2) = more[: len(early)], more[len(early) : len(early) + 3]
    out_master, out_moment1, out_moment2, out_own, unit, total = more[-6:]
    step = pl.program_id(0)
    slab_rows, lanes = out_own.shape

    @pl.when(step == 0)
    def _():
        down = lax.broadcasted_iota(jnp.int32, unit.shape, 0)
        unit[...] = (down == lax.broadcasted_iota(jnp.int32, unit.shape, 1)).astype(jnp.bfloat16)

    def upright(part):
        return lax.dot_general(
            unit[...], part, (((1,), (1,)), ((), ())), preferred_element_type=jnp.float32
        )

    if tail:

        @pl.when(step < 4)
        def _():
            total[...] = upright(back[...].reshape(lanes, slab_rows))

        @pl.when(step == 4)
        def _():
            shape = (lanes, 2 * lanes)
            feature = lax.broadcasted_iota(jnp.int32, shape, 0)
            line = lax.broadcasted_iota(jnp.int32, shape, 1)
            select = jnp.logical_and((line // 8) * 4 + line % 8 == feature, line % 8 < 4)
            part = jnp.dot(
                select.astype(jnp.bfloat16),
                rest[...].reshape(2 * lanes, slab_rows),
                preferred_element_type=jnp.float32,
            )
            total[...] = upright(part.astype(jnp.bfloat16))
    else:
        total[...] = upright(back[...].reshape(lanes, slab_rows))

    from_far = far[0][...].astype(jnp.float32)
    if len(early) == 2:
        from_far = jnp.where(step < early[1], from_far, far[1][...].astype(jnp.float32))
    gradient = total[...] + head[...].astype(jnp.float32) + from_far
    first = beta_first * moment1[...] + (1.0 - beta_first) * gradient
    second = beta_second * moment2[...] + (1.0 - beta_second) * gradient * gradient
    fresh = master[...] - (learn_rate / first_fix) * first / (
        jnp.sqrt(second * (1.0 / second_fix)) + adam_epsilon
    )
    out_master[...] = fresh
    out_moment1[...] = first
    out_moment2[...] = second
    out_own[...] = fresh.astype(jnp.bfloat16)


def adam(back, group, lanes, head, far, master, moment1, moment2, earlier=()):
    members, rows, slab_rows = back.shape
    quarter = master.shape[1]
    span = 512 if group == 0 else quarter - 512
    first = 512 * group // lanes
    tile = pl.BlockSpec((slab_rows, lanes), lambda i: (0, first + i))

    def far_spec(begin, array):
        last = array.shape[1] // lanes - 1
        return pl.BlockSpec((slab_rows, lanes), lambda i: (0, jnp.clip(first + i - begin, 0, last)))

    begins = [0, far[0].shape[1] // lanes][: len(far)]
    whole = jax.ShapeDtypeStruct(master.shape, jnp.float32)
    return pl.pallas_call(
        functools.partial(adam_kernel, [begin - first for begin in begins], span > 512),
        grid=(span // lanes,),
        in_specs=[
            pl.BlockSpec(
                (lanes // 16, 16, slab_rows), lambda i: (jnp.minimum(i, 512 // lanes - 1), group, 0)
            ),
            pl.BlockSpec((members, 8, slab_rows), lambda i: (0, rows // 8 - 1, 0)),
            tile,
            *[far_spec(*pair) for pair in zip(begins, far)],
            tile,
            tile,
            tile,
        ]
        + [pl.BlockSpec(memory_space=pl.ANY)] * len(earlier),
        out_specs=[tile, tile, tile, pl.BlockSpec((slab_rows, lanes), lambda i: (0, i))],
        out_shape=[whole, whole, whole, jax.ShapeDtypeStruct((slab_rows, span), jnp.bfloat16)],
        scratch_shapes=[
            pltpu.VMEM((slab_rows, slab_rows), jnp.bfloat16),
            pltpu.VMEM((slab_rows, lanes), jnp.float32),
        ],
        input_output_aliases={6 + len(far) + at: at for at in range(len(earlier))},
        compiler_params=pltpu.CompilerParams(vmem_limit_bytes=52 * MIB),
        cost_estimate=pl.CostEstimate(
            flops=4 * 128 * span * slab_rows,
            bytes_accessed=slab_rows * span * 36,
            transcendentals=slab_rows * span,
        ),
    )(back, back, head, *far, master, moment1, moment2, *earlier)


def place_kernel(count, place, *refs):
    parts, out = refs[:-1], refs[-1]
    quarter = out.shape[1] // 4
    for k in range(4):
        start = (place[0] ^ k) * quarter
        for at in range(count):
            part = parts[k * count + at]
            size = part.shape[1]
            out[:, pl.ds(pl.multiple_of(start, 128), size)] = part[...]
            start = start + size


def assemble(section, pieces):
    count = len(pieces[0])
    rows = pieces[0][0].shape[0]
    quarter = sum(part.shape[1] for part in pieces[0])
    some = 176
    parts = [part for piece in pieces for part in piece]
    return pl.pallas_call(
        functools.partial(place_kernel, count),
        grid_spec=pltpu.PrefetchScalarGridSpec(
            num_scalar_prefetch=1,
            grid=(-(-rows // some),),
            in_specs=[pl.BlockSpec((some, part.shape[1]), lambda i, place: (i, 0)) for part in parts],
            out_specs=pl.BlockSpec((some, 4 * quarter), lambda i, place: (i, 0)),
        ),
        out_shape=jax.ShapeDtypeStruct((rows, 4 * quarter), jnp.bfloat16),
        compiler_params=pltpu.CompilerParams(vmem_limit_bytes=20 * MIB),
        cost_estimate=pl.CostEstimate(
            flops=0, bytes_accessed=4 * rows * quarter * 4, transcendentals=0
        ),
    )(section.reshape(1), *parts)


def exchange(rows):
    return lax.all_to_all(rows, "vocab", split_axis=0, concat_axis=0, tiled=True)


def shards(token_grad, token_ids, block_counts, hidden, dlogits, master, moment1, moment2):
    section = lax.axis_index("section").astype(jnp.int32)
    quarter = token_grad.shape[1]
    slab_rows = master.shape[0]
    hidden_theirs = lax.ppermute(hidden, "section", CORE)
    dlogits_theirs = lax.ppermute(dlogits, "section", CORE)
    got = exchange(messages(block_counts, token_ids, token_grad))

    head, early, late = head_parts(section, hidden, dlogits, hidden_theirs, dlogits_theirs)
    got, late = lax.optimization_barrier((got, late))
    early = lax.ppermute(early, "section", ACROSS)
    late = lax.ppermute(late, "section", ACROSS)
    sums, early = lax.optimization_barrier((owner_sums(got, slab_rows), early))
    back = exchange(sums)

    *states, own_a = adam(back, 0, 256, head, [early], master, moment1, moment2)
    far_a = lax.ppermute(own_a, "section", ACROSS)
    core_a = lax.ppermute(own_a, "section", CORE)
    *states, own_b = adam(
        back, 1, 128, head, [early, late], master, moment1, moment2, earlier=states
    )
    turn_b, far_a = lax.optimization_barrier((own_b, far_a))
    far_b = lax.ppermute(turn_b, "section", ACROSS)
    core_b = lax.ppermute(own_b, "section", CORE)
    cross_a = lax.ppermute(far_a, "section", CORE)
    cross_b = lax.ppermute(far_b, "section", CORE)
    refreshed = assemble(
        section,
        ((own_a, own_b), (core_a, core_b), (far_a, far_b), (cross_a, cross_b)),
    )
    return (*states, refreshed)


def solution(mesh):
    placed = (
        P("vocab", "section"),
        P("vocab"),
        P("vocab", None),
        P("section", None),
        P("section", "vocab"),
        P("vocab", "section"),
        P("vocab", "section"),
        P("vocab", "section"),
    )
    return jax.shard_map(
        shards,
        mesh=mesh,
        in_specs=placed,
        out_specs=(
            P("vocab", "section"),
            P("vocab", "section"),
            P("vocab", "section"),
            P("vocab", None),
        ),
        check_vma=False,
    )
```

```python
import functools

import jax
import jax.numpy as jnp
from jax import lax
from jax.experimental import pallas as pl
from jax.experimental.pallas import tpu as pltpu
from jax.sharding import PartitionSpec as P

BLOCK = 128
MIB = 1024 * 1024


beta_first = 0.9
beta_second = 0.999
learn_rate = 0.01
adam_epsilon = 1e-08
first_fix = 1.0 - 0.9**10
second_fix = 1.0 - 0.999**10

CORE = ((0, 1), (1, 0), (2, 3), (3, 2))
ACROSS = ((0, 2), (2, 0), (1, 3), (3, 1))


def head_kernel(place, mine, theirs, hidden, hidden_theirs, own, early, late):
    half = pl.program_id(0)

    def product():
        return jnp.dot(mine[...], hidden[...], preferred_element_type=jnp.float32) + jnp.dot(
            theirs[...], hidden_theirs[...], preferred_element_type=jnp.float32
        )

    @pl.when(half == 0)
    def _():
        both = product().astype(jnp.bfloat16)
        early[...] = both[:, :640]
        late[...] = both[:, 640:]

    @pl.when(half == 1)
    def _():
        own[...] = product().astype(jnp.bfloat16)


def head_parts(section, hidden, dlogits, hidden_theirs, dlogits_theirs):
    tokens, rows = dlogits.shape
    quarter = hidden.shape[1] // 4
    left = pl.BlockSpec((rows, tokens), lambda h, place: (0, 0))
    right = pl.BlockSpec((tokens, quarter), lambda h, place: (0, place[0] ^ (2 - 2 * h)))
    shapes = [
        jax.ShapeDtypeStruct((rows, quarter), jnp.bfloat16),
        jax.ShapeDtypeStruct((rows, 640), jnp.bfloat16),
        jax.ShapeDtypeStruct((rows, quarter - 640), jnp.bfloat16),
    ]
    return pl.pallas_call(
        head_kernel,
        grid_spec=pltpu.PrefetchScalarGridSpec(
            num_scalar_prefetch=1,
            grid=(2,),
            in_specs=[left, left, right, right],
            out_specs=[pl.BlockSpec(shape.shape, lambda h, place: (0, 0)) for shape in shapes],
        ),
        out_shape=shapes,
        compiler_params=pltpu.CompilerParams(vmem_limit_bytes=58 * MIB),
        cost_estimate=pl.CostEstimate(
            flops=4 * tokens * rows * 2 * quarter,
            bytes_accessed=4 * tokens * (2 * quarter + rows) + 8 * rows * quarter,
            transcendentals=0,
        ),
    )(section.reshape(1), dlogits.T, dlogits_theirs.T, hidden, hidden_theirs)


SENDERS = 4


MAIN = 512


def sum_kernel(
    marks, got, out, acc, parts, tails, last, ids, keys, place, place_smem, sem
):
    step = pl.program_id(0)
    members, rows, _ = acc.shape
    senders = got.shape[0]
    blocks = got.shape[2] // BLOCK
    lane = lax.broadcasted_iota(jnp.int32, (1, BLOCK), 1)

    @pl.when(step == 0)
    def _():
        for member in range(members):
            mark = marks[member].astype(jnp.float32)
            numbers = mark[4:5] * 32.0 + mark[5:6] - 1.0
            owner = mark[6:7].astype(jnp.int32)
            spots = jnp.zeros((1, BLOCK), jnp.int32)
            key = jnp.full((1, BLOCK), -1, jnp.int32)
            for block in range(blocks):
                lanes = slice(block * BLOCK, (block + 1) * BLOCK)
                ids[member, block : block + 1] = numbers[:, lanes]
                spots = jnp.where(lane == block, owner[:, lanes], spots)
                key = jnp.where(lane // 8 == block, owner[:, lanes] * 8 + lane % 8, key)
            place[member : member + 1] = spots
            keys[member : member + 1] = key
        copy = pltpu.make_async_copy(place, place_smem, sem)
        copy.start()
        acc[...] = jnp.zeros_like(acc)
        copy.wait()

    slot = lax.broadcasted_iota(jnp.int32, (BLOCK, MAIN), 1).astype(jnp.float32)

    def add(sender):
        for block in range(blocks):
            spot = place_smem[step * senders + sender, block]
            acc[spot] += parts[sender * blocks + block]

    for sender in range(senders):
        columns = ids[step * senders + sender].T
        ends = []
        for block in range(blocks):
            part = got[sender, :, block * BLOCK : (block + 1) * BLOCK]
            column = columns[:, block : block + 1]
            one_hot = (slot == column).astype(jnp.bfloat16)
            parts[sender * blocks + block] = jnp.dot(
                part, one_hot, preferred_element_type=jnp.float32
            )
            end = jnp.where(lane // 8 == block, MAIN + lane % 8, -7).astype(jnp.float32)
            ends.append((end == column).astype(jnp.bfloat16))
        tails[step * senders + sender] = jnp.dot(
            got[sender], jnp.concatenate(ends, axis=0), preferred_element_type=jnp.float32
        ).astype(jnp.bfloat16)
        if sender > 0:
            add(sender - 1)
    add(senders - 1)

    @pl.when(step == pl.num_programs(0) - 1)
    def _():
        line = lax.broadcasted_iota(jnp.int32, (8 * members, BLOCK), 0)
        total = jnp.zeros((8 * members, rows), jnp.float32)
        for member in range(members):
            total += lax.dot_general(
                (line == keys[member : member + 1]).astype(jnp.bfloat16),
                tails[member],
                (((1,), (1,)), ((), ())),
                preferred_element_type=jnp.float32,
            )
        last[...] = jnp.zeros_like(last)
        last[:, :rows] = total
        upper = lax.broadcasted_iota(jnp.int32, (8, BLOCK), 0) < 4

        def leave(spot, carry):
            out[spot, :32] = acc[spot, :32].astype(jnp.bfloat16)
            tail = last[pl.ds(pl.multiple_of(8 * spot, 8), 8)]
            under = [pltpu.roll(tail, 4, 0), tail, jnp.zeros_like(tail), jnp.zeros_like(tail)]
            for at in range(4):
                lanes = slice(at * BLOCK, (at + 1) * BLOCK)
                out[spot, 32:, lanes] = jnp.where(upper, acc[spot, 32:, lanes], under[at]).astype(
                    jnp.bfloat16
                )
            return carry

        lax.fori_loop(0, members, leave, 0)


def owner_sums(got):
    members, rows, row_total = got.shape
    blocks = row_total // BLOCK
    shape = (members, rows, MAIN)
    return pl.pallas_call(
        sum_kernel,
        grid=(members // SENDERS,),
        in_specs=[
            pl.BlockSpec((members, 8, row_total), lambda i: (0, rows // 8 - 1, 0)),
            pl.BlockSpec((SENDERS, rows, row_total), lambda i: (i, 0, 0)),
        ],
        out_specs=pl.BlockSpec(shape, lambda i: (0, 0, 0)),
        out_shape=jax.ShapeDtypeStruct(shape, jnp.bfloat16),
        scratch_shapes=[
            pltpu.VMEM((members, rows, MAIN), jnp.float32),
            pltpu.VMEM((SENDERS * blocks, rows, MAIN), jnp.float32),
            pltpu.VMEM((members, rows, BLOCK), jnp.bfloat16),
            pltpu.VMEM((8 * members, BLOCK), jnp.float32),
            pltpu.VMEM((members, blocks, BLOCK), jnp.float32),
            pltpu.VMEM((members, BLOCK), jnp.int32),
            pltpu.VMEM((members, BLOCK), jnp.int32),
            pltpu.SMEM((members, BLOCK), jnp.int32),
            pltpu.SemaphoreType.DMA,
        ],
        compiler_params=pltpu.CompilerParams(vmem_limit_bytes=20 * MIB),
        cost_estimate=pl.CostEstimate(flops=0, bytes_accessed=0, transcendentals=0),
    )(got, got)


def turned(block):
    size = block.shape[1]
    down = lax.broadcasted_iota(jnp.int32, (size, size), 0)
    unit = (down == lax.broadcasted_iota(jnp.int32, (size, size), 1)).astype(jnp.bfloat16)
    return lax.dot_general(
        unit, block, (((1,), (1,)), ((), ())), preferred_element_type=jnp.float32
    ).astype(jnp.bfloat16)


def message_kernel(counts, ids, first, second, third, out, rest, marks):
    step = pl.program_id(0)
    blocks = ids.shape[0]

    @pl.when(step == 0)
    def _():
        owners = counts.shape[1]
        shape = (owners, owners)
        before = lax.broadcasted_iota(jnp.int32, shape, 0) <= lax.broadcasted_iota(
            jnp.int32, shape, 1
        )
        ends = jnp.dot(
            jnp.broadcast_to(counts[...].astype(jnp.float32), (8, owners)).astype(jnp.bfloat16),
            before.astype(jnp.bfloat16),
            preferred_element_type=jnp.float32,
        )
        at = lax.broadcasted_iota(jnp.int32, ends.shape, 0).astype(jnp.float32)
        owner = jnp.sum((ends <= at).astype(jnp.float32), axis=1, keepdims=True)
        owner = jnp.broadcast_to(owner, ids.shape)
        shifted = ids[...] + 1
        high = (shifted >> 5).astype(jnp.float32)
        low = (shifted & 31).astype(jnp.float32)
        marks[...] = jnp.zeros_like(marks)
        for block in range(blocks):
            lanes = slice(block * BLOCK, (block + 1) * BLOCK)
            row = slice(block, block + 1)
            marks[0:1, lanes] = high[row]
            marks[1:2, lanes] = low[row]
            marks[2:3, lanes] = owner[row]
        tail = turned(third[...]).astype(jnp.float32)
        for member in range(rest.shape[0]):
            both = jnp.concatenate([tail[member * 4 : member * 4 + 4], marks[0:4]], axis=0)
            rest[member] = both.astype(jnp.bfloat16)

    a = turned(first[...])
    b = turned(second[...])
    for member in range(8):
        out[member, :16] = a[member * 16 : member * 16 + 16]
        out[member, 16:32] = b[member * 16 : member * 16 + 16]
        out[member, 32:] = rest[step * 8 + member]


def messages(block_counts, token_ids, token_grad):
    row_total = token_grad.shape[0]
    blocks = row_total // BLOCK
    return pl.pallas_call(
        message_kernel,
        grid=(4,),
        in_specs=[
            pl.BlockSpec(block_counts.shape, lambda i: (0, 0)),
            pl.BlockSpec((blocks, BLOCK), lambda i: (0, 0)),
            pl.BlockSpec((row_total, 128), lambda i: (0, i)),
            pl.BlockSpec((row_total, 128), lambda i: (0, 4 + i)),
            pl.BlockSpec((row_total, 128), lambda i: (0, 8)),
        ],
        out_specs=pl.BlockSpec((8, 40, row_total), lambda i: (i, 0, 0)),
        out_shape=jax.ShapeDtypeStruct((32, 40, row_total), jnp.bfloat16),
        scratch_shapes=[
            pltpu.VMEM((32, 8, row_total), jnp.bfloat16),
            pltpu.VMEM((8, row_total), jnp.float32),
        ],
        compiler_params=pltpu.CompilerParams(vmem_limit_bytes=58 * MIB),
        cost_estimate=pl.CostEstimate(
            flops=2 * row_total * 1152 * 128,
            bytes_accessed=2 * row_total * (1152 + 1280),
            transcendentals=0,
        ),
    )(block_counts, token_ids.reshape(blocks, BLOCK), token_grad, token_grad, token_grad)


def adam_kernel(early, group, tail, back, rest, head, *more):
    far, (master, moment1, moment2) = more[: len(early)], more[len(early) : len(early) + 3]
    out_master, out_moment1, out_moment2, out_own, unit, total = more[-6:]
    step = pl.program_id(0)
    lanes = out_own.shape[1]
    upper = lax.broadcasted_iota(jnp.int32, (8, 128), 0) < 4
    lane = lax.broadcasted_iota(jnp.int32, (8, 128), 1)

    @pl.when(step == 0)
    def _():
        down = lax.broadcasted_iota(jnp.int32, unit.shape, 0)
        unit[...] = (down == lax.broadcasted_iota(jnp.int32, unit.shape, 1)).astype(jnp.bfloat16)

    def upright(part):
        return lax.dot_general(
            unit[...], part, (((1,), (1,)), ((), ())), preferred_element_type=jnp.float32
        )

    def end(member):
        ends = rest[member].astype(jnp.float32)
        return jnp.where(upper, pltpu.roll(ends[:, :128], 4, 0), ends[:, 128:256])

    def gather(members, width, start):
        found = jnp.zeros((8, 128), jnp.float32)
        for at, member in enumerate(members):
            turned_end = pltpu.roll(end(member), (width * at - start) % 128, 1)
            found = jnp.where(lane // width == at, turned_end, found)
        return found

    def whole_rows():
        total[:MAIN] = upright(back[...].reshape(lanes, MAIN))
        for at in range(lanes // 128):
            first = step * (lanes // 16) + 8 * at
            total[MAIN:, 128 * at : 128 * at + 128] = gather(
                [first + j for j in range(8)], 16, 16 * group
            )

    if tail:

        @pl.when(step < 4)
        def _():
            whole_rows()

        @pl.when(step == 4)
        def _():
            shape = (lanes, 2 * lanes)
            feature = lax.broadcasted_iota(jnp.int32, shape, 0)
            line = lax.broadcasted_iota(jnp.int32, shape, 1)
            select = jnp.logical_and((line // 8) * 4 + line % 8 == feature, line % 8 < 4)
            part = jnp.dot(
                select.astype(jnp.bfloat16),
                rest[...].reshape(2 * lanes, MAIN),
                preferred_element_type=jnp.float32,
            )
            total[:MAIN] = upright(part.astype(jnp.bfloat16))
            total[MAIN:] = gather(range(32), 4, 32)
    else:
        whole_rows()

    from_far = far[0][...].astype(jnp.float32)
    if len(early) == 2:
        from_far = jnp.where(step < early[1], from_far, far[1][...].astype(jnp.float32))
    gradient = total[...] + head[...].astype(jnp.float32) + from_far
    first = beta_first * moment1[...] + (1.0 - beta_first) * gradient
    second = beta_second * moment2[...] + (1.0 - beta_second) * gradient * gradient
    fresh = master[...] - (learn_rate / first_fix) * first / (
        jnp.sqrt(second * (1.0 / second_fix)) + adam_epsilon
    )
    out_master[...] = fresh
    out_moment1[...] = first
    out_moment2[...] = second
    out_own[...] = fresh.astype(jnp.bfloat16)


def adam(back, group, lanes, head, far, master, moment1, moment2, earlier=()):
    members, rows, _ = back.shape
    slab_rows, quarter = master.shape
    span = 512 if group == 0 else quarter - 512
    first = 512 * group // lanes
    tile = pl.BlockSpec((slab_rows, lanes), lambda i: (0, first + i))

    def far_spec(begin, array):
        last = array.shape[1] // lanes - 1
        return pl.BlockSpec((slab_rows, lanes), lambda i: (0, jnp.clip(first + i - begin, 0, last)))

    begins = [0, far[0].shape[1] // lanes][: len(far)]
    whole = jax.ShapeDtypeStruct(master.shape, jnp.float32)
    return pl.pallas_call(
        functools.partial(adam_kernel, [begin - first for begin in begins], group, span > 512),
        grid=(span // lanes,),
        in_specs=[
            pl.BlockSpec(
                (lanes // 16, 16, MAIN), lambda i: (jnp.minimum(i, 512 // lanes - 1), group, 0)
            ),
            pl.BlockSpec((members, 8, MAIN), lambda i: (0, rows // 8 - 1, 0)),
            tile,
            *[far_spec(*pair) for pair in zip(begins, far)],
            tile,
            tile,
            tile,
        ]
        + [pl.BlockSpec(memory_space=pl.ANY)] * len(earlier),
        out_specs=[tile, tile, tile, pl.BlockSpec((slab_rows, lanes), lambda i: (0, i))],
        out_shape=[whole, whole, whole, jax.ShapeDtypeStruct((slab_rows, span), jnp.bfloat16)],
        scratch_shapes=[
            pltpu.VMEM((MAIN, MAIN), jnp.bfloat16),
            pltpu.VMEM((slab_rows, lanes), jnp.float32),
        ],
        input_output_aliases={6 + len(far) + at: at for at in range(len(earlier))},
        compiler_params=pltpu.CompilerParams(vmem_limit_bytes=52 * MIB),
        cost_estimate=pl.CostEstimate(
            flops=4 * 128 * span * slab_rows,
            bytes_accessed=slab_rows * span * 36,
            transcendentals=slab_rows * span,
        ),
    )(back, back, head, *far, master, moment1, moment2, *earlier)


def place_kernel(count, place, *refs):
    parts, out = refs[:-1], refs[-1]
    quarter = out.shape[1] // 4
    for k in range(4):
        start = (place[0] ^ k) * quarter
        for at in range(count):
            part = parts[k * count + at]
            size = part.shape[1]
            out[:, pl.ds(pl.multiple_of(start, 128), size)] = part[...]
            start = start + size


def assemble(section, pieces):
    count = len(pieces[0])
    rows = pieces[0][0].shape[0]
    quarter = sum(part.shape[1] for part in pieces[0])
    some = 176
    parts = [part for piece in pieces for part in piece]
    return pl.pallas_call(
        functools.partial(place_kernel, count),
        grid_spec=pltpu.PrefetchScalarGridSpec(
            num_scalar_prefetch=1,
            grid=(-(-rows // some),),
            in_specs=[pl.BlockSpec((some, part.shape[1]), lambda i, place: (i, 0)) for part in parts],
            out_specs=pl.BlockSpec((some, 4 * quarter), lambda i, place: (i, 0)),
        ),
        out_shape=jax.ShapeDtypeStruct((rows, 4 * quarter), jnp.bfloat16),
        compiler_params=pltpu.CompilerParams(vmem_limit_bytes=20 * MIB),
        cost_estimate=pl.CostEstimate(
            flops=0, bytes_accessed=4 * rows * quarter * 4, transcendentals=0
        ),
    )(section.reshape(1), *parts)


def exchange(rows):
    return lax.all_to_all(rows, "vocab", split_axis=0, concat_axis=0, tiled=True)


def shards(token_grad, token_ids, block_counts, hidden, dlogits, master, moment1, moment2):
    section = lax.axis_index("section").astype(jnp.int32)
    hidden_theirs = lax.ppermute(hidden, "section", CORE)
    dlogits_theirs = lax.ppermute(dlogits, "section", CORE)
    got = exchange(messages(block_counts, token_ids, token_grad))

    head, early, late = head_parts(section, hidden, dlogits, hidden_theirs, dlogits_theirs)
    got, late = lax.optimization_barrier((got, late))
    early = lax.ppermute(early, "section", ACROSS)
    late = lax.ppermute(late, "section", ACROSS)
    sums, early = lax.optimization_barrier((owner_sums(got), early))
    back = exchange(sums)

    *states, own_a = adam(back, 0, 256, head, [early], master, moment1, moment2)
    far_a = lax.ppermute(own_a, "section", ACROSS)
    core_a = lax.ppermute(own_a, "section", CORE)
    *states, own_b = adam(
        back, 1, 128, head, [early, late], master, moment1, moment2, earlier=states
    )
    turn_b, far_a = lax.optimization_barrier((own_b, far_a))
    far_b = lax.ppermute(turn_b, "section", ACROSS)
    core_b = lax.ppermute(own_b, "section", CORE)
    cross_a = lax.ppermute(far_a, "section", CORE)
    cross_b = lax.ppermute(far_b, "section", CORE)
    refreshed = assemble(
        section,
        ((own_a, own_b), (core_a, core_b), (far_a, far_b), (cross_a, cross_b)),
    )
    return (*states, refreshed)


def solution(mesh):
    placed = (
        P("vocab", "section"),
        P("vocab"),
        P("vocab", None),
        P("section", None),
        P("section", "vocab"),
        P("vocab", "section"),
        P("vocab", "section"),
        P("vocab", "section"),
    )
    return jax.shard_map(
        shards,
        mesh=mesh,
        in_specs=placed,
        out_specs=(
            P("vocab", "section"),
            P("vocab", "section"),
            P("vocab", "section"),
            P("vocab", None),
        ),
        check_vma=False,
    )
```

```python
import functools

import jax
import jax.numpy as jnp
from jax import lax
from jax.experimental import pallas as pl
from jax.experimental.pallas import tpu as pltpu
from jax.sharding import PartitionSpec as P

BLOCK = 128
MIB = 1024 * 1024


beta_first = 0.9
beta_second = 0.999
learn_rate = 0.01
adam_epsilon = 1e-08
first_fix = 1.0 - 0.9**10
second_fix = 1.0 - 0.999**10

CORE = ((0, 1), (1, 0), (2, 3), (3, 2))
ACROSS = ((0, 2), (2, 0), (1, 3), (3, 1))


def head_kernel(place, mine, theirs, hidden, hidden_theirs, own, early, late):
    half = pl.program_id(0)

    def product():
        return jnp.dot(mine[...], hidden[...], preferred_element_type=jnp.float32) + jnp.dot(
            theirs[...], hidden_theirs[...], preferred_element_type=jnp.float32
        )

    @pl.when(half == 0)
    def _():
        both = product().astype(jnp.bfloat16)
        early[...] = both[:, :640]
        late[...] = both[:, 640:]

    @pl.when(half == 1)
    def _():
        own[...] = product().astype(jnp.bfloat16)


def head_parts(section, hidden, dlogits, hidden_theirs, dlogits_theirs):
    tokens, rows = dlogits.shape
    quarter = hidden.shape[1] // 4
    left = pl.BlockSpec((rows, tokens), lambda h, place: (0, 0))
    right = pl.BlockSpec((tokens, quarter), lambda h, place: (0, place[0] ^ (2 - 2 * h)))
    shapes = [
        jax.ShapeDtypeStruct((rows, quarter), jnp.bfloat16),
        jax.ShapeDtypeStruct((rows, 640), jnp.bfloat16),
        jax.ShapeDtypeStruct((rows, quarter - 640), jnp.bfloat16),
    ]
    return pl.pallas_call(
        head_kernel,
        grid_spec=pltpu.PrefetchScalarGridSpec(
            num_scalar_prefetch=1,
            grid=(2,),
            in_specs=[left, left, right, right],
            out_specs=[pl.BlockSpec(shape.shape, lambda h, place: (0, 0)) for shape in shapes],
        ),
        out_shape=shapes,
        compiler_params=pltpu.CompilerParams(vmem_limit_bytes=58 * MIB),
        cost_estimate=pl.CostEstimate(
            flops=4 * tokens * rows * 2 * quarter,
            bytes_accessed=4 * tokens * (2 * quarter + rows) + 8 * rows * quarter,
            transcendentals=0,
        ),
    )(section.reshape(1), dlogits.T, dlogits_theirs.T, hidden, hidden_theirs)


SENDERS = 8


MAIN = 512
SLOTS, SHIFT = 256, 8


def sum_kernel(marks, got, out, acc, parts, last, ids, highs, place, place_smem, sem):
    step = pl.program_id(0)
    members, rows = acc.shape[0], got.shape[1]
    senders = got.shape[0]
    blocks = got.shape[2] // BLOCK
    groups = acc.shape[1] // rows

    @pl.when(step == 0)
    def _():
        lane = lax.broadcasted_iota(jnp.int32, (1, BLOCK), 1)
        for member in range(members):
            mark = marks[member].astype(jnp.float32)
            numbers = (mark[4:5] * 32.0 + mark[5:6] - 1.0).astype(jnp.int32)
            owner = mark[6:7].astype(jnp.int32)
            low = jnp.where(numbers < 0, -1, numbers & (SLOTS - 1)).astype(jnp.float32)
            highs[member] = numbers >> SHIFT
            spots = jnp.zeros((1, BLOCK), jnp.int32)
            for block in range(blocks):
                lanes = slice(block * BLOCK, (block + 1) * BLOCK)
                ids[member, block : block + 1] = low[:, lanes]
                spots = jnp.where(lane == block, owner[:, lanes], spots)
            place[member : member + 1] = spots
        copy = pltpu.make_async_copy(place, place_smem, sem)
        copy.start()
        acc[...] = jnp.zeros_like(acc)
        copy.wait()

    slot = lax.broadcasted_iota(jnp.int32, (SLOTS, BLOCK), 0).astype(jnp.float32)

    def add(sender):
        for block in range(blocks):
            spot = place_smem[step * senders + sender, block]
            acc[spot] += parts[sender * blocks + block]

    for sender in range(senders):
        low = ids[step * senders + sender]
        high = highs[step * senders + sender]
        values = got[sender].astype(jnp.float32)
        masked = jnp.concatenate(
            [jnp.where(high == group, values, 0.0) for group in range(groups)], axis=0
        ).astype(jnp.bfloat16)
        for block in range(blocks):
            one_hot = (slot == low[block : block + 1]).astype(jnp.bfloat16)
            parts[sender * blocks + block] = lax.dot_general(
                masked[:, block * BLOCK : (block + 1) * BLOCK],
                one_hot,
                (((1,), (1,)), ((), ())),
                preferred_element_type=jnp.float32,
            )
        if sender > 0:
            add(sender - 1)
    add(senders - 1)

    @pl.when(step == pl.num_programs(0) - 1)
    def _():
        shape = (8, BLOCK)
        down = lax.broadcasted_iota(jnp.int32, shape, 0)
        unit = (down == lax.broadcasted_iota(jnp.int32, shape, 1)).astype(jnp.bfloat16)
        last[...] = jnp.zeros_like(last)
        for member in range(members):
            last[8 * member : 8 * member + 8, :rows] = lax.dot_general(
                unit,
                acc[member, (groups - 1) * rows :, :BLOCK].astype(jnp.bfloat16),
                (((1,), (1,)), ((), ())),
                preferred_element_type=jnp.float32,
            )
        upper = down < 4

        def leave(spot, carry):
            tail = last[pl.ds(pl.multiple_of(8 * spot, 8), 8)]
            under = [pltpu.roll(tail, 4, 0), tail, jnp.zeros_like(tail), jnp.zeros_like(tail)]
            for at in range(4):
                lanes = slice(at * BLOCK, (at + 1) * BLOCK)
                first = at * BLOCK // SLOTS * rows
                held = slice(at * BLOCK % SLOTS, at * BLOCK % SLOTS + BLOCK)
                top = acc[spot, first : first + 32, held]
                end = acc[spot, first + 32 : first + rows, held]
                out[spot, :32, lanes] = top.astype(jnp.bfloat16)
                out[spot, 32:, lanes] = jnp.where(upper, end, under[at]).astype(jnp.bfloat16)
            return carry

        lax.fori_loop(0, members, leave, 0)


def owner_sums(got):
    members, rows, row_total = got.shape
    blocks = row_total // BLOCK
    shape = (members, rows, MAIN)
    groups = MAIN // SLOTS + 1
    return pl.pallas_call(
        sum_kernel,
        grid=(members // SENDERS,),
        in_specs=[
            pl.BlockSpec((members, 8, row_total), lambda i: (0, rows // 8 - 1, 0)),
            pl.BlockSpec((SENDERS, rows, row_total), lambda i: (i, 0, 0)),
        ],
        out_specs=pl.BlockSpec(shape, lambda i: (0, 0, 0)),
        out_shape=jax.ShapeDtypeStruct(shape, jnp.bfloat16),
        scratch_shapes=[
            pltpu.VMEM((members, groups * rows, SLOTS), jnp.float32),
            pltpu.VMEM((SENDERS * blocks, groups * rows, SLOTS), jnp.float32),
            pltpu.VMEM((8 * members, BLOCK), jnp.float32),
            pltpu.VMEM((members, blocks, BLOCK), jnp.float32),
            pltpu.VMEM((members, 1, row_total), jnp.int32),
            pltpu.VMEM((members, BLOCK), jnp.int32),
            pltpu.SMEM((members, BLOCK), jnp.int32),
            pltpu.SemaphoreType.DMA,
        ],
        compiler_params=pltpu.CompilerParams(vmem_limit_bytes=20 * MIB),
        cost_estimate=pl.CostEstimate(flops=0, bytes_accessed=0, transcendentals=0),
    )(got, got)


def turned(block):
    size = block.shape[1]
    down = lax.broadcasted_iota(jnp.int32, (size, size), 0)
    unit = (down == lax.broadcasted_iota(jnp.int32, (size, size), 1)).astype(jnp.bfloat16)
    return lax.dot_general(
        unit, block, (((1,), (1,)), ((), ())), preferred_element_type=jnp.float32
    ).astype(jnp.bfloat16)


def message_kernel(counts, ids, first, second, third, out, rest, marks):
    step = pl.program_id(0)
    blocks = ids.shape[0]

    @pl.when(step == 0)
    def _():
        owners = counts.shape[1]
        shape = (owners, owners)
        before = lax.broadcasted_iota(jnp.int32, shape, 0) <= lax.broadcasted_iota(
            jnp.int32, shape, 1
        )
        ends = jnp.dot(
            jnp.broadcast_to(counts[...].astype(jnp.float32), (8, owners)).astype(jnp.bfloat16),
            before.astype(jnp.bfloat16),
            preferred_element_type=jnp.float32,
        )
        at = lax.broadcasted_iota(jnp.int32, ends.shape, 0).astype(jnp.float32)
        owner = jnp.sum((ends <= at).astype(jnp.float32), axis=1, keepdims=True)
        owner = jnp.broadcast_to(owner, ids.shape)
        shifted = ids[...] + 1
        high = (shifted >> 5).astype(jnp.float32)
        low = (shifted & 31).astype(jnp.float32)
        marks[...] = jnp.zeros_like(marks)
        for block in range(blocks):
            lanes = slice(block * BLOCK, (block + 1) * BLOCK)
            row = slice(block, block + 1)
            marks[0:1, lanes] = high[row]
            marks[1:2, lanes] = low[row]
            marks[2:3, lanes] = owner[row]
        tail = turned(third[...]).astype(jnp.float32)
        for member in range(rest.shape[0]):
            both = jnp.concatenate([tail[member * 4 : member * 4 + 4], marks[0:4]], axis=0)
            rest[member] = both.astype(jnp.bfloat16)

    a = turned(first[...])
    b = turned(second[...])
    for member in range(8):
        out[member, :16] = a[member * 16 : member * 16 + 16]
        out[member, 16:32] = b[member * 16 : member * 16 + 16]
        out[member, 32:] = rest[step * 8 + member]


def messages(block_counts, token_ids, token_grad):
    row_total = token_grad.shape[0]
    blocks = row_total // BLOCK
    return pl.pallas_call(
        message_kernel,
        grid=(4,),
        in_specs=[
            pl.BlockSpec(block_counts.shape, lambda i: (0, 0)),
            pl.BlockSpec((blocks, BLOCK), lambda i: (0, 0)),
            pl.BlockSpec((row_total, 128), lambda i: (0, i)),
            pl.BlockSpec((row_total, 128), lambda i: (0, 4 + i)),
            pl.BlockSpec((row_total, 128), lambda i: (0, 8)),
        ],
        out_specs=pl.BlockSpec((8, 40, row_total), lambda i: (i, 0, 0)),
        out_shape=jax.ShapeDtypeStruct((32, 40, row_total), jnp.bfloat16),
        scratch_shapes=[
            pltpu.VMEM((32, 8, row_total), jnp.bfloat16),
            pltpu.VMEM((8, row_total), jnp.float32),
        ],
        compiler_params=pltpu.CompilerParams(vmem_limit_bytes=58 * MIB),
        cost_estimate=pl.CostEstimate(
            flops=2 * row_total * 1152 * 128,
            bytes_accessed=2 * row_total * (1152 + 1280),
            transcendentals=0,
        ),
    )(block_counts, token_ids.reshape(blocks, BLOCK), token_grad, token_grad, token_grad)


def adam_kernel(early, group, tail, back, rest, head, *more):
    far, (master, moment1, moment2) = more[: len(early)], more[len(early) : len(early) + 3]
    out_master, out_moment1, out_moment2, out_own, unit, total = more[-6:]
    step = pl.program_id(0)
    lanes = out_own.shape[1]
    upper = lax.broadcasted_iota(jnp.int32, (8, 128), 0) < 4
    lane = lax.broadcasted_iota(jnp.int32, (8, 128), 1)

    @pl.when(step == 0)
    def _():
        down = lax.broadcasted_iota(jnp.int32, unit.shape, 0)
        unit[...] = (down == lax.broadcasted_iota(jnp.int32, unit.shape, 1)).astype(jnp.bfloat16)

    def upright(part):
        return lax.dot_general(
            unit[...], part, (((1,), (1,)), ((), ())), preferred_element_type=jnp.float32
        )

    def end(member):
        ends = rest[member].astype(jnp.float32)
        return jnp.where(upper, pltpu.roll(ends[:, :128], 4, 0), ends[:, 128:256])

    def gather(members, width, start):
        found = jnp.zeros((8, 128), jnp.float32)
        for at, member in enumerate(members):
            turned_end = pltpu.roll(end(member), (width * at - start) % 128, 1)
            found = jnp.where(lane // width == at, turned_end, found)
        return found

    def whole_rows():
        total[:MAIN] = upright(back[...].reshape(lanes, MAIN))
        for at in range(lanes // 128):
            first = step * (lanes // 16) + 8 * at
            total[MAIN:, 128 * at : 128 * at + 128] = gather(
                [first + j for j in range(8)], 16, 16 * group
            )

    if tail:

        @pl.when(step < 4)
        def _():
            whole_rows()

        @pl.when(step == 4)
        def _():
            shape = (lanes, 2 * lanes)
            feature = lax.broadcasted_iota(jnp.int32, shape, 0)
            line = lax.broadcasted_iota(jnp.int32, shape, 1)
            select = jnp.logical_and((line // 8) * 4 + line % 8 == feature, line % 8 < 4)
            part = jnp.dot(
                select.astype(jnp.bfloat16),
                rest[...].reshape(2 * lanes, MAIN),
                preferred_element_type=jnp.float32,
            )
            total[:MAIN] = upright(part.astype(jnp.bfloat16))
            total[MAIN:] = gather(range(32), 4, 32)
    else:
        whole_rows()

    from_far = far[0][...].astype(jnp.float32)
    if len(early) == 2:
        from_far = jnp.where(step < early[1], from_far, far[1][...].astype(jnp.float32))
    gradient = total[...] + head[...].astype(jnp.float32) + from_far
    first = beta_first * moment1[...] + (1.0 - beta_first) * gradient
    second = beta_second * moment2[...] + (1.0 - beta_second) * gradient * gradient
    fresh = master[...] - (learn_rate / first_fix) * first / (
        jnp.sqrt(second * (1.0 / second_fix)) + adam_epsilon
    )
    out_master[...] = fresh
    out_moment1[...] = first
    out_moment2[...] = second
    out_own[...] = fresh.astype(jnp.bfloat16)


def adam(back, group, lanes, head, far, master, moment1, moment2, earlier=()):
    members, rows, _ = back.shape
    slab_rows, quarter = master.shape
    span = 512 if group == 0 else quarter - 512
    first = 512 * group // lanes
    tile = pl.BlockSpec((slab_rows, lanes), lambda i: (0, first + i))

    def far_spec(begin, array):
        last = array.shape[1] // lanes - 1
        return pl.BlockSpec((slab_rows, lanes), lambda i: (0, jnp.clip(first + i - begin, 0, last)))

    begins = [0, far[0].shape[1] // lanes][: len(far)]
    whole = jax.ShapeDtypeStruct(master.shape, jnp.float32)
    return pl.pallas_call(
        functools.partial(adam_kernel, [begin - first for begin in begins], group, span > 512),
        grid=(span // lanes,),
        in_specs=[
            pl.BlockSpec(
                (lanes // 16, 16, MAIN), lambda i: (jnp.minimum(i, 512 // lanes - 1), group, 0)
            ),
            pl.BlockSpec((members, 8, MAIN), lambda i: (0, rows // 8 - 1, 0)),
            tile,
            *[far_spec(*pair) for pair in zip(begins, far)],
            tile,
            tile,
            tile,
        ]
        + [pl.BlockSpec(memory_space=pl.ANY)] * len(earlier),
        out_specs=[tile, tile, tile, pl.BlockSpec((slab_rows, lanes), lambda i: (0, i))],
        out_shape=[whole, whole, whole, jax.ShapeDtypeStruct((slab_rows, span), jnp.bfloat16)],
        scratch_shapes=[
            pltpu.VMEM((MAIN, MAIN), jnp.bfloat16),
            pltpu.VMEM((slab_rows, lanes), jnp.float32),
        ],
        input_output_aliases={6 + len(far) + at: at for at in range(len(earlier))},
        compiler_params=pltpu.CompilerParams(vmem_limit_bytes=52 * MIB),
        cost_estimate=pl.CostEstimate(
            flops=4 * 128 * span * slab_rows,
            bytes_accessed=slab_rows * span * 36,
            transcendentals=slab_rows * span,
        ),
    )(back, back, head, *far, master, moment1, moment2, *earlier)


def place_kernel(count, place, *refs):
    parts, out = refs[:-1], refs[-1]
    quarter = out.shape[1] // 4
    for k in range(4):
        start = (place[0] ^ k) * quarter
        for at in range(count):
            part = parts[k * count + at]
            size = part.shape[1]
            out[:, pl.ds(pl.multiple_of(start, 128), size)] = part[...]
            start = start + size


def assemble(section, pieces):
    count = len(pieces[0])
    rows = pieces[0][0].shape[0]
    quarter = sum(part.shape[1] for part in pieces[0])
    some = 176
    parts = [part for piece in pieces for part in piece]
    return pl.pallas_call(
        functools.partial(place_kernel, count),
        grid_spec=pltpu.PrefetchScalarGridSpec(
            num_scalar_prefetch=1,
            grid=(-(-rows // some),),
            in_specs=[pl.BlockSpec((some, part.shape[1]), lambda i, place: (i, 0)) for part in parts],
            out_specs=pl.BlockSpec((some, 4 * quarter), lambda i, place: (i, 0)),
        ),
        out_shape=jax.ShapeDtypeStruct((rows, 4 * quarter), jnp.bfloat16),
        compiler_params=pltpu.CompilerParams(vmem_limit_bytes=20 * MIB),
        cost_estimate=pl.CostEstimate(
            flops=0, bytes_accessed=4 * rows * quarter * 4, transcendentals=0
        ),
    )(section.reshape(1), *parts)


def exchange(rows):
    return lax.all_to_all(rows, "vocab", split_axis=0, concat_axis=0, tiled=True)


def shards(token_grad, token_ids, block_counts, hidden, dlogits, master, moment1, moment2):
    section = lax.axis_index("section").astype(jnp.int32)
    hidden_theirs = lax.ppermute(hidden, "section", CORE)
    dlogits_theirs = lax.ppermute(dlogits, "section", CORE)
    got = exchange(messages(block_counts, token_ids, token_grad))

    head, early, late = head_parts(section, hidden, dlogits, hidden_theirs, dlogits_theirs)
    got, late = lax.optimization_barrier((got, late))
    early = lax.ppermute(early, "section", ACROSS)
    late = lax.ppermute(late, "section", ACROSS)
    sums, early = lax.optimization_barrier((owner_sums(got), early))
    back = exchange(sums)

    *states, own_a = adam(back, 0, 256, head, [early], master, moment1, moment2)
    far_a = lax.ppermute(own_a, "section", ACROSS)
    core_a = lax.ppermute(own_a, "section", CORE)
    *states, own_b = adam(
        back, 1, 128, head, [early, late], master, moment1, moment2, earlier=states
    )
    turn_b, far_a = lax.optimization_barrier((own_b, far_a))
    far_b = lax.ppermute(turn_b, "section", ACROSS)
    core_b = lax.ppermute(own_b, "section", CORE)
    cross_a = lax.ppermute(far_a, "section", CORE)
    far_b, core_a, core_b, cross_a = lax.optimization_barrier((far_b, core_a, core_b, cross_a))
    cross_b = lax.ppermute(far_b, "section", CORE)
    refreshed = assemble(
        section,
        ((own_a, own_b), (core_a, core_b), (far_a, far_b), (cross_a, cross_b)),
    )
    return (*states, refreshed)


def solution(mesh):
    placed = (
        P("vocab", "section"),
        P("vocab"),
        P("vocab", None),
        P("section", None),
        P("section", "vocab"),
        P("vocab", "section"),
        P("vocab", "section"),
        P("vocab", "section"),
    )
    return jax.shard_map(
        shards,
        mesh=mesh,
        in_specs=placed,
        out_specs=(
            P("vocab", "section"),
            P("vocab", "section"),
            P("vocab", "section"),
            P("vocab", None),
        ),
        check_vma=False,
    )
```

```python
import functools

import jax
import jax.numpy as jnp
from jax import lax
from jax.experimental import pallas as pl
from jax.experimental.pallas import tpu as pltpu
from jax.sharding import PartitionSpec as P

BLOCK = 128
MIB = 1024 * 1024


beta_first = 0.9
beta_second = 0.999
learn_rate = 0.01
adam_epsilon = 1e-08
first_fix = 1.0 - 0.9**10
second_fix = 1.0 - 0.999**10

CORE = ((0, 1), (1, 0), (2, 3), (3, 2))
ACROSS = ((0, 2), (2, 0), (1, 3), (3, 1))


def head_kernel(place, mine, theirs, hidden, hidden_theirs, own, early, late):
    half = pl.program_id(0)

    def product():
        return jnp.dot(mine[...], hidden[...], preferred_element_type=jnp.float32) + jnp.dot(
            theirs[...], hidden_theirs[...], preferred_element_type=jnp.float32
        )

    @pl.when(half == 0)
    def _():
        both = product().astype(jnp.bfloat16)
        early[...] = both[:, :640]
        late[...] = both[:, 640:]

    @pl.when(half == 1)
    def _():
        own[...] = product().astype(jnp.bfloat16)


def head_parts(section, hidden, dlogits, hidden_theirs, dlogits_theirs):
    tokens, rows = dlogits.shape
    quarter = hidden.shape[1] // 4
    left = pl.BlockSpec((rows, tokens), lambda h, place: (0, 0))
    right = pl.BlockSpec((tokens, quarter), lambda h, place: (0, place[0] ^ (2 - 2 * h)))
    shapes = [
        jax.ShapeDtypeStruct((rows, quarter), jnp.bfloat16),
        jax.ShapeDtypeStruct((rows, 640), jnp.bfloat16),
        jax.ShapeDtypeStruct((rows, quarter - 640), jnp.bfloat16),
    ]
    return pl.pallas_call(
        head_kernel,
        grid_spec=pltpu.PrefetchScalarGridSpec(
            num_scalar_prefetch=1,
            grid=(2,),
            in_specs=[left, left, right, right],
            out_specs=[pl.BlockSpec(shape.shape, lambda h, place: (0, 0)) for shape in shapes],
        ),
        out_shape=shapes,
        compiler_params=pltpu.CompilerParams(vmem_limit_bytes=58 * MIB),
        cost_estimate=pl.CostEstimate(
            flops=4 * tokens * rows * 2 * quarter,
            bytes_accessed=4 * tokens * (2 * quarter + rows) + 8 * rows * quarter,
            transcendentals=0,
        ),
    )(section.reshape(1), dlogits.T, dlogits_theirs.T, hidden, hidden_theirs)


SENDERS = 8


MAIN = 512
SLOTS, SHIFT = 256, 8


def sum_kernel(marks, got, out, acc, parts, last, ids, highs, place, place_smem, sem):
    step = pl.program_id(0)
    members, rows = acc.shape[0], got.shape[1]
    senders = got.shape[0]
    blocks = got.shape[2] // BLOCK
    groups = acc.shape[1] // rows

    @pl.when(step == 0)
    def _():
        lane = lax.broadcasted_iota(jnp.int32, (1, BLOCK), 1)
        for member in range(members):
            mark = marks[member].astype(jnp.float32)
            numbers = (mark[4:5] * 32.0 + mark[5:6] - 1.0).astype(jnp.int32)
            owner = mark[6:7].astype(jnp.int32)
            low = jnp.where(numbers < 0, -1, numbers & (SLOTS - 1)).astype(jnp.float32)
            highs[member] = numbers >> SHIFT
            spots = jnp.zeros((1, BLOCK), jnp.int32)
            for block in range(blocks):
                lanes = slice(block * BLOCK, (block + 1) * BLOCK)
                ids[member, block : block + 1] = low[:, lanes]
                spots = jnp.where(lane == block, owner[:, lanes], spots)
            place[member : member + 1] = spots
        copy = pltpu.make_async_copy(place, place_smem, sem)
        copy.start()
        acc[...] = jnp.zeros_like(acc)
        copy.wait()

    slot = lax.broadcasted_iota(jnp.int32, (SLOTS, BLOCK), 0).astype(jnp.float32)

    def add(sender):
        for block in range(blocks):
            spot = place_smem[step * senders + sender, block]
            acc[spot] += parts[sender * blocks + block]

    for sender in range(senders):
        low = ids[step * senders + sender]
        high = highs[step * senders + sender]
        values = got[sender].astype(jnp.float32)
        masked = jnp.concatenate(
            [jnp.where(high == group, values, 0.0) for group in range(groups)], axis=0
        ).astype(jnp.bfloat16)
        for block in range(blocks):
            one_hot = (slot == low[block : block + 1]).astype(jnp.bfloat16)
            parts[sender * blocks + block] = lax.dot_general(
                masked[:, block * BLOCK : (block + 1) * BLOCK],
                one_hot,
                (((1,), (1,)), ((), ())),
                preferred_element_type=jnp.float32,
            )
        if sender > 0:
            add(sender - 1)
    add(senders - 1)

    @pl.when(step == pl.num_programs(0) - 1)
    def _():
        shape = (8, BLOCK)
        down = lax.broadcasted_iota(jnp.int32, shape, 0)
        unit = (down == lax.broadcasted_iota(jnp.int32, shape, 1)).astype(jnp.bfloat16)
        last[...] = jnp.zeros_like(last)
        for member in range(members):
            last[8 * member : 8 * member + 8, :rows] = lax.dot_general(
                unit,
                acc[member, (groups - 1) * rows :, :BLOCK].astype(jnp.bfloat16),
                (((1,), (1,)), ((), ())),
                preferred_element_type=jnp.float32,
            )
        upper = down < 4

        def leave(spot, carry):
            tail = last[pl.ds(pl.multiple_of(8 * spot, 8), 8)]
            under = [pltpu.roll(tail, 4, 0), tail, jnp.zeros_like(tail), jnp.zeros_like(tail)]
            for at in range(4):
                lanes = slice(at * BLOCK, (at + 1) * BLOCK)
                first = at * BLOCK // SLOTS * rows
                held = slice(at * BLOCK % SLOTS, at * BLOCK % SLOTS + BLOCK)
                top = acc[spot, first : first + 32, held]
                end = acc[spot, first + 32 : first + rows, held]
                out[spot, :32, lanes] = top.astype(jnp.bfloat16)
                out[spot, 32:, lanes] = jnp.where(upper, end, under[at]).astype(jnp.bfloat16)
            return carry

        lax.fori_loop(0, members, leave, 0)


def owner_sums(got):
    members, rows, row_total = got.shape
    blocks = row_total // BLOCK
    shape = (members, rows, MAIN)
    groups = MAIN // SLOTS + 1
    return pl.pallas_call(
        sum_kernel,
        grid=(members // SENDERS,),
        in_specs=[
            pl.BlockSpec((members, 8, row_total), lambda i: (0, rows // 8 - 1, 0)),
            pl.BlockSpec((SENDERS, rows, row_total), lambda i: (i, 0, 0)),
        ],
        out_specs=pl.BlockSpec(shape, lambda i: (0, 0, 0)),
        out_shape=jax.ShapeDtypeStruct(shape, jnp.bfloat16),
        scratch_shapes=[
            pltpu.VMEM((members, groups * rows, SLOTS), jnp.float32),
            pltpu.VMEM((SENDERS * blocks, groups * rows, SLOTS), jnp.float32),
            pltpu.VMEM((8 * members, BLOCK), jnp.float32),
            pltpu.VMEM((members, blocks, BLOCK), jnp.float32),
            pltpu.VMEM((members, 1, row_total), jnp.int32),
            pltpu.VMEM((members, BLOCK), jnp.int32),
            pltpu.SMEM((members, BLOCK), jnp.int32),
            pltpu.SemaphoreType.DMA,
        ],
        compiler_params=pltpu.CompilerParams(vmem_limit_bytes=20 * MIB),
        cost_estimate=pl.CostEstimate(flops=0, bytes_accessed=0, transcendentals=0),
    )(got, got)


def turned(block):
    size = block.shape[1]
    down = lax.broadcasted_iota(jnp.int32, (size, size), 0)
    unit = (down == lax.broadcasted_iota(jnp.int32, (size, size), 1)).astype(jnp.bfloat16)
    return lax.dot_general(
        unit, block, (((1,), (1,)), ((), ())), preferred_element_type=jnp.float32
    ).astype(jnp.bfloat16)


def message_kernel(counts, ids, first, second, third, out, rest, marks):
    step = pl.program_id(0)
    blocks = ids.shape[0]

    @pl.when(step == 0)
    def _():
        owners = counts.shape[1]
        shape = (owners, owners)
        before = lax.broadcasted_iota(jnp.int32, shape, 0) <= lax.broadcasted_iota(
            jnp.int32, shape, 1
        )
        ends = jnp.dot(
            jnp.broadcast_to(counts[...].astype(jnp.float32), (8, owners)).astype(jnp.bfloat16),
            before.astype(jnp.bfloat16),
            preferred_element_type=jnp.float32,
        )
        at = lax.broadcasted_iota(jnp.int32, ends.shape, 0).astype(jnp.float32)
        owner = jnp.sum((ends <= at).astype(jnp.float32), axis=1, keepdims=True)
        owner = jnp.broadcast_to(owner, ids.shape)
        shifted = ids[...] + 1
        high = (shifted >> 5).astype(jnp.float32)
        low = (shifted & 31).astype(jnp.float32)
        marks[...] = jnp.zeros_like(marks)
        for block in range(blocks):
            lanes = slice(block * BLOCK, (block + 1) * BLOCK)
            row = slice(block, block + 1)
            marks[0:1, lanes] = high[row]
            marks[1:2, lanes] = low[row]
            marks[2:3, lanes] = owner[row]
        tail = turned(third[...]).astype(jnp.float32)
        for member in range(rest.shape[0]):
            both = jnp.concatenate([tail[member * 4 : member * 4 + 4], marks[0:4]], axis=0)
            rest[member] = both.astype(jnp.bfloat16)

    a = turned(first[...])
    b = turned(second[...])
    for member in range(8):
        out[member, :16] = a[member * 16 : member * 16 + 16]
        out[member, 16:32] = b[member * 16 : member * 16 + 16]
        out[member, 32:] = rest[step * 8 + member]


def messages(block_counts, token_ids, token_grad):
    row_total = token_grad.shape[0]
    blocks = row_total // BLOCK
    return pl.pallas_call(
        message_kernel,
        grid=(4,),
        in_specs=[
            pl.BlockSpec(block_counts.shape, lambda i: (0, 0)),
            pl.BlockSpec((blocks, BLOCK), lambda i: (0, 0)),
            pl.BlockSpec((row_total, 128), lambda i: (0, i)),
            pl.BlockSpec((row_total, 128), lambda i: (0, 4 + i)),
            pl.BlockSpec((row_total, 128), lambda i: (0, 8)),
        ],
        out_specs=pl.BlockSpec((8, 40, row_total), lambda i: (i, 0, 0)),
        out_shape=jax.ShapeDtypeStruct((32, 40, row_total), jnp.bfloat16),
        scratch_shapes=[
            pltpu.VMEM((32, 8, row_total), jnp.bfloat16),
            pltpu.VMEM((8, row_total), jnp.float32),
        ],
        compiler_params=pltpu.CompilerParams(vmem_limit_bytes=58 * MIB),
        cost_estimate=pl.CostEstimate(
            flops=2 * row_total * 1152 * 128,
            bytes_accessed=2 * row_total * (1152 + 1280),
            transcendentals=0,
        ),
    )(block_counts, token_ids.reshape(blocks, BLOCK), token_grad, token_grad, token_grad)


def adam_kernel(early, group, tail, back, rest, head, *more):
    far, (master, moment1, moment2) = more[: len(early)], more[len(early) : len(early) + 3]
    out_master, out_moment1, out_moment2, out_own, unit, total = more[-6:]
    step = pl.program_id(0)
    lanes = out_own.shape[1]
    upper = lax.broadcasted_iota(jnp.int32, (8, 128), 0) < 4
    lane = lax.broadcasted_iota(jnp.int32, (8, 128), 1)

    @pl.when(step == 0)
    def _():
        down = lax.broadcasted_iota(jnp.int32, unit.shape, 0)
        unit[...] = (down == lax.broadcasted_iota(jnp.int32, unit.shape, 1)).astype(jnp.bfloat16)

    def upright(part):
        return lax.dot_general(
            unit[...], part, (((1,), (1,)), ((), ())), preferred_element_type=jnp.float32
        )

    def end(member):
        ends = rest[member].astype(jnp.float32)
        return jnp.where(upper, pltpu.roll(ends[:, :128], 4, 0), ends[:, 128:256])

    def gather(members, width, start):
        found = jnp.zeros((8, 128), jnp.float32)
        for at, member in enumerate(members):
            turned_end = pltpu.roll(end(member), (width * at - start) % 128, 1)
            found = jnp.where(lane // width == at, turned_end, found)
        return found

    def whole_rows():
        total[:MAIN] = upright(back[...].reshape(lanes, MAIN))
        for at in range(lanes // 128):
            first = step * (lanes // 16) + 8 * at
            total[MAIN:, 128 * at : 128 * at + 128] = gather(
                [first + j for j in range(8)], 16, 16 * group
            )

    if tail:

        @pl.when(step < 4)
        def _():
            whole_rows()

        @pl.when(step == 4)
        def _():
            shape = (lanes, 2 * lanes)
            feature = lax.broadcasted_iota(jnp.int32, shape, 0)
            line = lax.broadcasted_iota(jnp.int32, shape, 1)
            select = jnp.logical_and((line // 8) * 4 + line % 8 == feature, line % 8 < 4)
            part = jnp.dot(
                select.astype(jnp.bfloat16),
                rest[...].reshape(2 * lanes, MAIN),
                preferred_element_type=jnp.float32,
            )
            total[:MAIN] = upright(part.astype(jnp.bfloat16))
            total[MAIN:] = gather(range(32), 4, 32)
    else:
        whole_rows()

    from_far = far[0][...].astype(jnp.float32)
    if len(early) == 2:
        from_far = jnp.where(step < early[1], from_far, far[1][...].astype(jnp.float32))
    gradient = total[...] + head[...].astype(jnp.float32) + from_far
    first = beta_first * moment1[...] + (1.0 - beta_first) * gradient
    second = beta_second * moment2[...] + (1.0 - beta_second) * gradient * gradient
    fresh = master[...] - (learn_rate / first_fix) * first / (
        jnp.sqrt(second * (1.0 / second_fix)) + adam_epsilon
    )
    out_master[...] = fresh
    out_moment1[...] = first
    out_moment2[...] = second
    out_own[...] = fresh.astype(jnp.bfloat16)


def adam(back, group, lanes, head, far, master, moment1, moment2, earlier=()):
    members, rows, _ = back.shape
    slab_rows, quarter = master.shape
    span = 512 if group == 0 else quarter - 512
    first = 512 * group // lanes
    tile = pl.BlockSpec((slab_rows, lanes), lambda i: (0, first + i))

    def far_spec(begin, array):
        last = array.shape[1] // lanes - 1
        return pl.BlockSpec((slab_rows, lanes), lambda i: (0, jnp.clip(first + i - begin, 0, last)))

    begins = [0, far[0].shape[1] // lanes][: len(far)]
    whole = jax.ShapeDtypeStruct(master.shape, jnp.float32)
    return pl.pallas_call(
        functools.partial(adam_kernel, [begin - first for begin in begins], group, span > 512),
        grid=(span // lanes,),
        in_specs=[
            pl.BlockSpec(
                (lanes // 16, 16, MAIN), lambda i: (jnp.minimum(i, 512 // lanes - 1), group, 0)
            ),
            pl.BlockSpec((members, 8, MAIN), lambda i: (0, rows // 8 - 1, 0)),
            tile,
            *[far_spec(*pair) for pair in zip(begins, far)],
            tile,
            tile,
            tile,
        ]
        + [pl.BlockSpec(memory_space=pl.ANY)] * len(earlier),
        out_specs=[tile, tile, tile, pl.BlockSpec((slab_rows, lanes), lambda i: (0, i))],
        out_shape=[whole, whole, whole, jax.ShapeDtypeStruct((slab_rows, span), jnp.bfloat16)],
        scratch_shapes=[
            pltpu.VMEM((MAIN, MAIN), jnp.bfloat16),
            pltpu.VMEM((slab_rows, lanes), jnp.float32),
        ],
        input_output_aliases={6 + len(far) + at: at for at in range(len(earlier))},
        compiler_params=pltpu.CompilerParams(vmem_limit_bytes=49 * MIB),
        cost_estimate=pl.CostEstimate(
            flops=4 * 128 * span * slab_rows,
            bytes_accessed=slab_rows * span * 36,
            transcendentals=slab_rows * span,
        ),
    )(back, back, head, *far, master, moment1, moment2, *earlier)


def place_kernel(count, place, *refs):
    parts, out = refs[:-1], refs[-1]
    quarter = out.shape[1] // 4
    for k in range(4):
        start = (place[0] ^ k) * quarter
        for at in range(count):
            part = parts[k * count + at]
            size = part.shape[1]
            out[:, pl.ds(pl.multiple_of(start, 128), size)] = part[...]
            start = start + size


def assemble(section, pieces):
    count = len(pieces[0])
    rows = pieces[0][0].shape[0]
    quarter = sum(part.shape[1] for part in pieces[0])
    some = 176
    parts = [part for piece in pieces for part in piece]
    return pl.pallas_call(
        functools.partial(place_kernel, count),
        grid_spec=pltpu.PrefetchScalarGridSpec(
            num_scalar_prefetch=1,
            grid=(-(-rows // some),),
            in_specs=[pl.BlockSpec((some, part.shape[1]), lambda i, place: (i, 0)) for part in parts],
            out_specs=pl.BlockSpec((some, 4 * quarter), lambda i, place: (i, 0)),
        ),
        out_shape=jax.ShapeDtypeStruct((rows, 4 * quarter), jnp.bfloat16),
        compiler_params=pltpu.CompilerParams(vmem_limit_bytes=20 * MIB),
        cost_estimate=pl.CostEstimate(
            flops=0, bytes_accessed=4 * rows * quarter * 4, transcendentals=0
        ),
    )(section.reshape(1), *parts)


def exchange(rows):
    return lax.all_to_all(rows, "vocab", split_axis=0, concat_axis=0, tiled=True)


def shards(token_grad, token_ids, block_counts, hidden, dlogits, master, moment1, moment2):
    section = lax.axis_index("section").astype(jnp.int32)
    hidden_theirs = lax.ppermute(hidden, "section", CORE)
    dlogits_theirs = lax.ppermute(dlogits, "section", CORE)
    got = exchange(messages(block_counts, token_ids, token_grad))

    head, early, late = head_parts(section, hidden, dlogits, hidden_theirs, dlogits_theirs)
    got, late = lax.optimization_barrier((got, late))
    early = lax.ppermute(early, "section", ACROSS)
    late = lax.ppermute(late, "section", ACROSS)
    sums, early = lax.optimization_barrier((owner_sums(got), early))
    back = exchange(sums)

    *states, own_a = adam(back, 0, 256, head, [early], master, moment1, moment2)
    far_a = lax.ppermute(own_a, "section", ACROSS)
    core_a = lax.ppermute(own_a, "section", CORE)
    *states, own_b = adam(
        back, 1, 128, head, [early, late], master, moment1, moment2, earlier=states
    )
    turn_b, far_a = lax.optimization_barrier((own_b, far_a))
    far_b = lax.ppermute(turn_b, "section", ACROSS)
    core_b = lax.ppermute(own_b, "section", CORE)
    cross_a = lax.ppermute(far_a, "section", CORE)
    far_b, core_a, core_b, cross_a = lax.optimization_barrier((far_b, core_a, core_b, cross_a))
    cross_b = lax.ppermute(far_b, "section", CORE)
    refreshed = assemble(
        section,
        ((own_a, own_b), (core_a, core_b), (far_a, far_b), (cross_a, cross_b)),
    )
    return (*states, refreshed)


def solution(mesh):
    placed = (
        P("vocab", "section"),
        P("vocab"),
        P("vocab", None),
        P("section", None),
        P("section", "vocab"),
        P("vocab", "section"),
        P("vocab", "section"),
        P("vocab", "section"),
    )
    return jax.shard_map(
        shards,
        mesh=mesh,
        in_specs=placed,
        out_specs=(
            P("vocab", "section"),
            P("vocab", "section"),
            P("vocab", "section"),
            P("vocab", None),
        ),
        check_vma=False,
    )
```
